512 devices in a mesh: dp: 32 (over y_hi, z), owner: 16 (over y_lo, x, core).
Axes of the slice: x: 4, y: 4 (y_hi: 2, y_lo: 2; y = y_hi * 2 + y_lo), z: 16, core: 2. Of those that a mesh axis runs over, the one named last changes fastest.
Arguments:
- gate_pre: bfloat16 [12288, 16, 6, 128], P('dp', 'owner'), may hold values from -6 to 6
- up_pre: bfloat16 [12288, 16, 6, 128], P('dp', 'owner'), may hold values from -6 to 6
- out_grad: bfloat16 [12288, 2560], P('dp'), may hold values from -6 to 6
- down_weight: bfloat16 [16, 2560, 6, 128], P('owner', 'dp'), may hold values from -0.125 to 0.125
- old_first: float32 [16, 2560, 9, 128], P('owner', 'dp'), may hold values from -8 to 8
- old_second: float32 [16, 2560, 9, 128], P('owner', 'dp'), may hold values from 0.5 to 16
- old_owner: int32 [54], replicated, may hold values from 0 to 7, as said below
- new_owner: int32 [54], replicated, may hold values from 0 to 15, as said below
Outputs:
- d_gate: bfloat16 [12288, 16, 6, 128], P('dp', 'owner')
- d_up: bfloat16 [12288, 16, 6, 128], P('dp', 'owner')
- new_first: float32 [16, 2560, 6, 128], P('owner', 'dp')
- new_second: float32 [16, 2560, 6, 128], P('owner', 'dp')
- step_dir: float32 [16, 2560, 6, 128], P('owner', 'dp')
The draws below stay inside these ranges and needn't reach their ends.
Inputs may be any that keep to these rules, and one draw needn't show every extreme that they name: `old_owner`: only owners 0 to 7 hold slabs; each holds at most 9 slabs and one holds exactly 9. `new_owner`: each owner holds at most 6 slabs and one holds exactly 6.
All inputs are finite; a program needn't handle non-finite values.
Results may differ from the reference program's by a relative error of at most 0.0075.
Values may be sent and summed in bfloat16 or wider, within the bound.
A program may use at most 128 MiB of HBM per device.

```python
import math
import jax
import jax.numpy as jnp
from jax import lax

D = 2560
SLAB = 128
TOK_DEV = 384
TOKENS = 12288
NSLAB = 54
CAP = 6
CAP_OLD = 9
N_DP = 32
N_OWNER = 16


def assign(key, groups, capacity):
    shuffled = jax.random.permutation(jax.random.fold_in(key, 11), NSLAB)
    busiest = jax.random.randint(jax.random.fold_in(key, 12), (), 0, groups)
    position = jnp.arange(NSLAB, dtype=jnp.int32)
    others = (position - capacity) % (groups - 1)
    others = others + (others >= busiest).astype(jnp.int32)
    owners_of = jnp.where(position < capacity, busiest, others).astype(jnp.int32)
    return jnp.zeros((NSLAB,), jnp.int32).at[shuffled].set(owners_of)


def draw_old_owner(key, part):
    key = jax.random.fold_in(key, 1)
    return assign(key, N_OWNER // 2, CAP_OLD)


def draw_new_owner(key, part):
    key = jax.random.fold_in(key, 2)
    return assign(key, N_OWNER, CAP)


def with_spikes(entries, key, source, target, shards_of, factor):
    owner, partner = [(jnp.arange(entries.shape[dim]) // (entries.shape[dim] // shards_of)).reshape([-1 if axis == dim else 1 for axis in range(entries.ndim)]) for dim in (source, target)]
    chosen = jax.random.permutation(key, shards_of)[partner]
    strong = (owner == chosen) | (owner == (partner + shards_of // 2) % shards_of)
    return jnp.where(strong, factor * entries, entries)


def block_scale(own_key, shape, cuts, least, high):
    level = 1.0
    for dim, parts in cuts:
        heights = jax.random.uniform(jax.random.fold_in(jax.random.fold_in(own_key, 6), dim), (parts,), jnp.float32, least / len(cuts), high / len(cuts))
        level = level * jnp.repeat(jnp.exp(heights), shape[dim] // parts).reshape((-1,) + (1,) * (len(shape) - 1 - dim))
    return level


def noise(rng, dims, width, most, pieces=(), kind=jnp.bfloat16):
    values = width * jax.random.normal(rng, dims, jnp.float32)
    if pieces:
        values = values * block_scale(rng, dims, pieces, -0.22, 0.18)
    return jnp.clip(values, -most, most).astype(kind)


def bell_draw_with(rng, dims, width, most, shards, heavy, held_as=jnp.bfloat16):
    drawn = width * jax.random.normal(rng, dims, jnp.float32)
    if shards:
        drawn = drawn * block_scale(rng, dims, shards, -0.22, 0.18)
    return jnp.clip(with_spikes(drawn, jax.random.fold_in(rng, 3), *heavy), -most, most).astype(held_as)


def setup_inputs(seed: int = 0) -> dict:
    splits = jax.random.split(jax.random.key(seed), 9)
    gate_pre = noise(splits[0], (TOKENS, N_OWNER, CAP, SLAB), 1.0, 6.0, ((0, 32), (1, 16)))
    up_pre = noise(splits[1], (TOKENS, N_OWNER, CAP, SLAB), 1.0, 6.0, ((0, 32), (1, 16)))
    out_grad = bell_draw_with(splits[2], (TOKENS, D), 1.0, 6.0, ((0, 32),), (0, 1, 32, 2.75))
    down_weight = noise(splits[3], (N_OWNER, D, CAP, SLAB), D ** -0.5, 0.125, ((0, 16), (1, 32)))
    old_first = noise(splits[4], (N_OWNER, D, CAP_OLD, SLAB), 2.0, 8.0, ((0, 16), (1, 32)), jnp.float32)
    old_second = jnp.clip(jnp.exp(math.log(16.0) - 3.465736 * jax.random.uniform(splits[5], (N_OWNER, D, CAP_OLD, SLAB), jnp.float32) ** block_scale(splits[5], (N_OWNER, D, CAP_OLD, SLAB), ((0, 16), (1, 32)), -0.2, 0.2)), 0.5, 16.0)
    old_owner = draw_old_owner(jax.random.fold_in(splits[8], 71), 0)
    new_owner = draw_new_owner(jax.random.fold_in(splits[8], 71), 0)
    return {"gate_pre": gate_pre, "up_pre": up_pre, "out_grad": out_grad, "down_weight": down_weight, "old_first": old_first, "old_second": old_second, "old_owner": old_owner, "new_owner": new_owner}


def slot_ranks(owner_map, groups):
    onehot = (owner_map[:, None] == jnp.arange(groups, dtype=jnp.int32)[None, :]).astype(jnp.int32)
    before = jnp.cumsum(onehot, axis=0) - onehot
    return (lax.optimization_barrier(jnp.sum(before * onehot, axis=1)).astype(jnp.int32), lax.optimization_barrier(jnp.sum(onehot, axis=0)).astype(jnp.int32))

def reference(gate_pre, up_pre, out_grad, down_weight, old_first, old_second, old_owner, new_owner):
    new_rank, new_count = slot_ranks(new_owner, N_OWNER)
    old_rank, old_count = slot_ranks(old_owner, N_OWNER)
    live = (jnp.arange(CAP, dtype=jnp.int32)[None, :] < new_count[:, None]).astype(jnp.float32)
    slab_ids = jnp.arange(NSLAB, dtype=jnp.int32)
    matches = (new_owner[None, None, :] == jnp.arange(N_OWNER, dtype=jnp.int32)[:, None, None]) & (new_rank[None, None, :] == jnp.arange(CAP, dtype=jnp.int32)[None, :, None])
    slab_at = lax.optimization_barrier(jnp.sum(jnp.where(matches, slab_ids[None, None, :], 0), axis=2)).astype(jnp.int32)
    source_owner = old_owner[slab_at]
    source_slot = old_rank[slab_at]
    prior_first = jnp.transpose(old_first[source_owner, :, source_slot, :], (0, 2, 1, 3))
    prior_second = jnp.transpose(old_second[source_owner, :, source_slot, :], (0, 2, 1, 3))
    gate32 = gate_pre.astype(jnp.float32)
    up32 = up_pre.astype(jnp.float32)
    sigmoid_gate = jax.nn.sigmoid(gate32)
    hidden = (gate32 * sigmoid_gate * up32).astype(jnp.bfloat16)

    def per_owner(owner_index):
        hidden_slab = lax.dynamic_index_in_dim(hidden, owner_index, 1, keepdims=False).reshape(TOKENS, CAP * SLAB)
        weight_slab = lax.dynamic_index_in_dim(down_weight, owner_index, 0, keepdims=False).reshape(D, CAP * SLAB)
        slab_grad = jnp.dot(out_grad, weight_slab, preferred_element_type=jnp.float32)
        partial_value = jnp.einsum('etd,etf->edf', out_grad.reshape(N_DP, TOK_DEV, D).astype(jnp.float32), hidden_slab.reshape(N_DP, TOK_DEV, CAP * SLAB).astype(jnp.float32))
        partial_value = lax.optimization_barrier(partial_value.astype(jnp.bfloat16)).astype(jnp.float32)
        return (slab_grad, lax.optimization_barrier(jnp.sum(partial_value, axis=0)))
    slab_grads, summed = lax.map(per_owner, jnp.arange(N_OWNER, dtype=jnp.int32))
    hidden_grad = jnp.transpose(slab_grads.reshape(N_OWNER, TOKENS, CAP, SLAB), (1, 0, 2, 3))
    hidden_grad = hidden_grad * live[None, :, :, None]
    d_gate = (hidden_grad * up32 * sigmoid_gate * (1.0 + gate32 * (1.0 - sigmoid_gate))).astype(jnp.bfloat16)
    d_up = (hidden_grad * gate32 * sigmoid_gate).astype(jnp.bfloat16)
    gradient = summed.reshape(N_OWNER, D, CAP, SLAB) * TOKENS ** (-0.5)
    mask = live[:, None, :, None]
    first = 0.9 * prior_first + 0.1 * gradient
    second = 0.95 * prior_second + 0.05 * gradient * gradient
    step_dir = first / (1.0 - 0.9 ** 20) / (jnp.sqrt(second / (1.0 - 0.95 ** 20)) + 1e-08)
    return (d_gate, d_up, first * mask, second * mask, step_dir * mask)
```

```python
import functools

import jax
import jax.numpy as jnp
from jax import lax
from jax.experimental import pallas as pl
from jax.experimental.pallas import tpu as pltpu
from jax.sharding import PartitionSpec as P

MESH = pl.DeviceIdType.MESH
BF, F32 = jnp.bfloat16, jnp.float32
NZ, NY, NX = 16, 4, 4
HOPS = 8
CAP, CAP_OLD, SLAB = 6, 9, 128
TOK, WIDTH = 384, 2560
HALF = WIDTH // 2
ROWS = WIDTH // 32
COLS = CAP * SLAB
SUB = COLS // 2
UNIT = TOK // 8
GB = 256
N_SLAB = 54
LR1, LR2 = 0.9, 0.95

SEM = {}


def _number(*names):
    for n in names:
        SEM[n] = len(SEM)


for _s in range(HOPS):
    for _d in range(2):
        for _k in range(2):
            _number(("ag", _d, _s, _k), ("rs", _d, _s, _k))
_number(("og",), ("ogx", 0), ("ogx", 1), ("ogx", 2), *[("ogc", i) for i in range(4)])
for _r in range(2):
    for _d in range(2):
        _number(("hid", _d, _r), ("hg", _d, _r))
for _i in range(2):
    _number(("my", _i), ("mx", 0, _i), ("mx", 1, _i), ("mf", _i))
    _number(*[("mc", j, _i) for j in range(4)])


def body(
    gate, up, og, w, m1, m2, old_map, new_map,
    dg_out, du_out, nf_out, ns_out, sd_out,
    gate_v, up_v, fg, fu, m1_v, m2_v, og_v, hid, hgs, hgr, hg_own,
    wb, gb, rsb, mb, grad, dg_v, du_v, nf_v, ns_v, sd_v,
    ssem, rsem, lsem,
):
    dp, ow = lax.axis_index("dp"), lax.axis_index("owner")
    hi, z = dp // NZ, dp % NZ
    lo, x, core = ow // 8, (ow // 2) % NX, ow % 2
    y = hi * 2 + lo

    def dev(y_, x_, z_, c_):
        return ((y_ // 2) * NZ + z_, (y_ % 2) * 8 + x_ * 2 + c_)

    zn = (dev(y, x, (z + 1) % NZ, core), dev(y, x, (z + NZ - 1) % NZ, core))
    far = dev((y + 2) % NY, x, z, core)
    lows = dev((y // 2) * 2 + 1 - lo, x, z, core)
    xn = (dev(y, (x + 1) % NX, z, core), dev(y, (x + NX - 1) % NX, z, core))
    cn = dev(y, x, z, 1 - core)
    other = dev((y + NY - 1 + 2 * lo) % NY, x, z, core)

    started = []

    def copy(name, src, dst, device):
        i = SEM[name]
        return pltpu.make_async_remote_copy(
            src_ref=src, dst_ref=dst, send_sem=ssem.at[i], recv_sem=rsem.at[i],
            device_id=device, device_id_type=MESH,
        )

    def send(name, src, dst, device):
        c = copy(name, src, dst, device)
        c.start()
        started.append(c)

    def arrived(name, dst, device):
        copy(name, dst, dst, device).wait_recv()

    def local(i, src, dst):
        return pltpu.make_async_copy(src, dst, lsem.at[i])

    def rows_of(t):
        return pl.ds(pl.multiple_of(t * ROWS, 16), ROWS)

    def sub(k):
        return pl.ds(k * SUB, SUB)

    mine_d = pl.ds(pl.multiple_of(hi * HALF, 128), HALF)
    other_d = pl.ds(pl.multiple_of((1 - hi) * HALF, 128), HALF)

    loads_w = [local(i, w.at[i], wb.at[rows_of(z), pl.ds(i * SLAB, SLAB)]) for i in range(CAP)]
    load_gate, load_up = local(6, gate, gate_v), local(7, up, up_v)
    load_og = local(8, og.at[:, mine_d], og_v.at[pl.ds(0, TOK)])
    load_m = [local(9, m1, m1_v), local(10, m2, m2_v)]
    for c in [*loads_w, load_gate, load_up, load_og, *load_m]:
        c.start()

    barrier = pltpu.get_barrier_semaphore()
    for n in (*zn, *xn, cn, far, other, lows):
        pl.semaphore_signal(barrier, inc=1, device_id=n, device_id_type=MESH)
    pl.semaphore_wait(barrier, 8)

    def unit(x_, c_):
        return pl.ds(pl.multiple_of((x_ * 2 + c_) * UNIT, 16), UNIT)

    def og_part(x_, c_):
        return og_v.at[pl.ds(pl.multiple_of(TOK + (x_ * 2 + c_) * UNIT, 16), UNIT)]

    send(("og",), og.at[unit(x, core), other_d], og_part(x, core), other)

    def hops(d, k):
        return HOPS if d == k else HOPS - 1

    def ag_slot(d, s):
        return (z + NZ - s) % NZ if d == 0 else (z + s) % NZ

    def ag_tick(s):
        for k in range(2):
            for d in range(2):
                if 0 < s <= hops(d, k):
                    dst = wb.at[rows_of(ag_slot(d, s)), sub(k)]
                    arrived(("ag", d, s - 1, k), dst, zn[d])
                if s < hops(d, k):
                    ref = wb.at[rows_of(ag_slot(d, s)), sub(k)]
                    send(("ag", d, s, k), ref, ref, zn[d])

    def rs_dest(d, s, k):
        n = hops(d, k)
        return (z + n - s) % NZ if d == 0 else (z + NZ - n + s) % NZ

    def rs_tick(s):
        for k in range(2):
            for d in range(2):
                if s >= hops(d, k):
                    continue
                mine = gb.at[rows_of(rs_dest(d, s, k)), sub(k)]
                if s == 0:
                    src = mine
                else:
                    src = rsb.at[d, s - 1, :, sub(k)]
                    arrived(("rs", d, s - 1, k), src, zn[d])
                    src[...] = (src[...].astype(F32) + mine[...].astype(F32)).astype(BF)
                send(("rs", d, s, k), src, rsb.at[d, s, :, sub(k)], zn[d])

    for c in loads_w:
        c.wait()
    ag_tick(0)

    load_gate.wait()
    load_up.wait()
    step = 64

    def hidden_rows(first):
        for slot in range(CAP):

            @pl.loop(0, TOK // 2 // step)
            def _(i):
                r = pl.ds(pl.multiple_of(first + i * step, step), step)
                g = gate_v[slot, r, :].astype(F32)
                u = up_v[slot, r, :].astype(F32)
                sig = jax.nn.sigmoid(g)
                gs = g * sig
                hid[r, pl.ds(slot * SLAB, SLAB)] = (gs * u).astype(BF)
                fu[slot, r, :] = gs
                fg[slot, r, :] = u * sig * (1.0 + g * (1.0 - sig))

    def half(r):
        return pl.ds(r * (TOK // 2), TOK // 2)

    def partner(r):
        return pl.ds(TOK + r * (TOK // 2), TOK // 2)

    for r in range(2):
        hidden_rows(r * (TOK // 2))
        for d in range(2):
            send(("hid", d, r), hid.at[half(r), sub(d)], hid.at[partner(r), sub(d)], far)

    me = x * 2 + core

    for c in load_m:
        c.wait()

    def to_y(i):
        ref = mb.at[me, i]
        return copy(("my", i), ref, ref, lows)

    @pl.when(lo == 0)
    def _():
        @pl.loop(0, CAP_OLD)
        def _(j):
            mb[me, 0, j] = m1_v[j].astype(BF)
            mb[me, 1, j] = m2_v[j].astype(BF)

        for i in range(2):
            to_y(i).start()

    ag_tick(1)

    def og_to(name, x_, device):
        send(name, og_part(x_, core), og_part(x_, core), device)

    x1, x2, x3 = (x + 1) % NX, (x + 2) % NX, (x + 3) % NX
    arrived(("og",), og_part(x, core), other)
    og_to(("ogx", 0), x, xn[0])
    og_to(("ogx", 1), x, xn[1])
    og_to(("ogc", 0), x, cn)

    ag_tick(2)

    arrived(("ogx", 0), og_part(x3, core), xn[0])
    og_to(("ogx", 2), x3, xn[0])
    og_to(("ogc", 1), x3, cn)
    arrived(("ogx", 1), og_part(x1, core), xn[1])
    og_to(("ogc", 2), x1, cn)

    ag_tick(3)

    @pl.when(lo == 1)
    def _():
        for i in range(2):
            to_y(i).wait_recv()

    def mom(x_, i):
        return mb.at[x_ * 2 + core, i]

    def mom_to(name, x_, i, device):
        send(name, mom(x_, i), mom(x_, i), device)

    for i in range(2):
        for d in range(2):
            mom_to(("mx", d, i), x, i, xn[d])
        mom_to(("mc", 0, i), x, i, cn)

    ag_tick(4)
    arrived(("ogx", 2), og_part(x2, core), xn[0])
    og_to(("ogc", 3), x2, cn)
    ag_tick(5)
    for i, x_ in enumerate((x, x3, x1, x2)):
        arrived(("ogc", i), og_part(x_, 1 - core), cn)
    load_og.wait()
    for r in range(2):
        for d in range(2):
            arrived(("hid", d, r), hid.at[partner(r), sub(d)], far)

    def grad_block(i):
        part = lax.dot_general(
            og_v[:, pl.ds(i * GB, GB)], hid[...], (((0,), (0,)), ((), ())),
            preferred_element_type=F32,
        )
        gb[pl.ds(i * GB, GB), :] = part.astype(BF)

    grad_block(0)
    ag_tick(6)
    grad_block(1)
    grad_block(2)
    ag_tick(7)
    grad_block(3)
    grad_block(4)
    rs_tick(0)
    ag_tick(8)

    for d, x_ in enumerate((x3, x1)):
        for i in range(2):
            arrived(("mx", d, i), mom(x_, i), xn[d])
        mom_to(("mf", d), x_, d, xn[d])
        for i in range(2):
            mom_to(("mc", 1 + d, i), x_, i, cn)

    def hidden_grad(first, out):
        @pl.loop(0, 3)
        def _(j):
            cols = pl.ds(pl.multiple_of(j * 256, 256), 256)
            out[:, cols] = jnp.dot(
                og_v[pl.ds(first, TOK), :], wb[:, cols], preferred_element_type=F32
            ).astype(out.dtype)

    hidden_grad(TOK, hgs)
    for r in range(2):
        for d in range(2):
            send(("hg", d, r), hgs.at[half(r), sub(d)], hgr.at[half(r), sub(d)], far)
    rs_tick(1)
    hidden_grad(0, hg_own)

    same = (N_SLAB, N_SLAB)
    lane, row = lax.broadcasted_iota(jnp.int32, same, 1), lax.broadcasted_iota(jnp.int32, same, 0)
    diagonal, earlier = lane == row, row < lane

    def owners_ranks(ref):
        across = jnp.broadcast_to(ref[...], same)
        down = jnp.sum(jnp.where(diagonal, across, 0), axis=1, keepdims=True)
        rank = jnp.sum(jnp.where((across == down) & earlier, 1, 0), axis=0, keepdims=True)
        return ref[...], rank

    old_own, old_rank = owners_ranks(old_map)
    new_own, new_rank = owners_ranks(new_map)
    slots = []
    for k in range(CAP):
        here = (new_own == ow) & (new_rank == k)
        slots.append(
            tuple(jnp.sum(jnp.where(here, v, 0)) for v in (old_own, old_rank, jnp.ones_like(old_own)))
        )

    rs_tick(2)

    rs_tick(3)
    for d in range(2):
        arrived(("mf", d), mom(x2, d), xn[d])
        mom_to(("mc", 3, d), x2, d, cn)
    rs_tick(4)
    rs_tick(5)
    rs_tick(6)

    for r in range(2):
        for d in range(2):
            arrived(("hg", d, r), hgr.at[half(r), sub(d)], far)
    for k in range(CAP):
        live = slots[k][2].astype(F32)

        @pl.loop(0, TOK // step)
        def _(i):
            r = pl.ds(pl.multiple_of(i * step, step), step)
            c = pl.ds(k * SLAB, SLAB)
            hg = (hg_own[r, c] + hgr[r, c].astype(F32)) * live
            dg_v[k, r, :] = (hg * fg[k, r, :]).astype(BF)
            du_v[k, r, :] = (hg * fu[k, r, :]).astype(BF)

    out_d = [local(11, dg_v, dg_out), local(12, du_v, du_out)]
    for c in out_d:
        c.start()

    rs_tick(7)

    for j, x_ in enumerate((x, x3, x1, x2)):
        for i in range(2):
            ref = mb.at[x_ * 2 + 1 - core, i]
            arrived(("mc", j, i), ref, cn)

    for k in range(2):
        total = gb[rows_of(z), sub(k)].astype(F32)
        for d in range(2):
            last = hops(d, k) - 1
            ref = rsb.at[d, last, :, sub(k)]
            arrived(("rs", d, last, k), ref, zn[d])
            total += ref[...].astype(F32)
        grad[:, sub(k)] = total * (TOK * 32) ** (-0.5)

    for k in range(CAP):
        q, j, n = slots[k]
        live = n.astype(F32)
        g = grad[:, pl.ds(k * SLAB, SLAB)]
        m = (LR1 * mb[q, 0, j].astype(F32) + 0.1 * g) * live
        s = (LR2 * mb[q, 1, j].astype(F32) + 0.05 * g * g) * live
        nf_v[k] = m
        ns_v[k] = s
        sd_v[k] = m / (1.0 - LR1**20) / (jnp.sqrt(s / (1.0 - LR2**20)) + 1e-08)

    out_m = [local(13, nf_v, nf_out), local(14, ns_v, ns_out), local(15, sd_v, sd_out)]
    for c in out_m:
        c.start()

    @pl.when(lo == 0)
    def _():
        for i in range(2):
            to_y(i).wait_send()

    for c in started:
        c.wait_send()
    for c in (*out_d, *out_m):
        c.wait()


def per_device(gate, up, og, w, m1, m2, old_map, new_map):
    hbm = pl.BlockSpec(memory_space=pl.ANY)
    vmem = pl.BlockSpec(memory_space=pltpu.VMEM)
    act = (CAP, TOK, SLAB)
    state = (CAP, ROWS, SLAB)
    old = (CAP_OLD, ROWS, SLAB)
    V = pltpu.VMEM
    outs = pl.pallas_call(
        body,
        out_shape=[jax.ShapeDtypeStruct(act, BF)] * 2 + [jax.ShapeDtypeStruct(state, F32)] * 3,
        in_specs=[hbm] * 6 + [vmem] * 2,
        out_specs=[hbm] * 5,
        scratch_shapes=[
            V(act, BF), V(act, BF), V(act, F32), V(act, F32), V(old, F32), V(old, F32),
            V((2 * TOK, HALF), BF), V((2 * TOK, COLS), BF),
            V((TOK, COLS), BF), V((TOK, COLS), BF), V((TOK, COLS), F32),
            V((HALF, COLS), BF), V((HALF, COLS), BF), V((2, HOPS, ROWS, COLS), BF),
            V((8, 2, *old), BF), V((ROWS, COLS), F32),
            V(act, BF), V(act, BF), V(state, F32), V(state, F32), V(state, F32),
            pltpu.SemaphoreType.DMA((len(SEM),)), pltpu.SemaphoreType.DMA((len(SEM),)),
            pltpu.SemaphoreType.DMA((16,)),
        ],
        compiler_params=pltpu.CompilerParams(
            collective_id=0, has_side_effects=True, vmem_limit_bytes=56 << 20
        ),
        cost_estimate=pl.CostEstimate(flops=6 * 10**9, bytes_accessed=12 * 10**6, transcendentals=0),
        name="step",
    )(
        gate[:, 0].transpose(1, 0, 2),
        up[:, 0].transpose(1, 0, 2),
        og,
        w[0].transpose(1, 0, 2),
        m1[0].transpose(1, 0, 2),
        m2[0].transpose(1, 0, 2),
        old_map[None],
        new_map[None],
    )
    dg, du, nf, ns, sd = outs
    return (
        dg.transpose(1, 0, 2)[:, None],
        du.transpose(1, 0, 2)[:, None],
        nf.transpose(1, 0, 2)[None],
        ns.transpose(1, 0, 2)[None],
        sd.transpose(1, 0, 2)[None],
    )


def solution(mesh):
    act, state = P("dp", "owner", None, None), P("owner", "dp", None, None)
    return jax.shard_map(
        per_device,
        mesh=mesh,
        in_specs=(act, act, P("dp", None), state, state, state, P(), P()),
        out_specs=(act, act, state, state, state),
        check_vma=False,
    )
```

```python
import functools

import jax
import jax.numpy as jnp
from jax import lax
from jax.experimental import pallas as pl
from jax.experimental.pallas import tpu as pltpu
from jax.sharding import PartitionSpec as P

MESH = pl.DeviceIdType.MESH
BF, F32 = jnp.bfloat16, jnp.float32
NZ, NY, NX = 16, 4, 4
HOPS = 8
CAP, CAP_OLD, SLAB = 6, 9, 128
TOK, WIDTH = 384, 2560
HALF = WIDTH // 2
ROWS = WIDTH // 32
COLS = CAP * SLAB
SUBS = 3
SUB = COLS // SUBS
UNIT = TOK // 8
GB = 256
N_SLAB = 54
LR1, LR2 = 0.9, 0.95

RECV, SEND = {}, {}


def _number(*names):
    for n in names:
        RECV[n], SEND[n] = len(set(RECV.values())), len(set(SEND.values()))


for _s in range(HOPS):
    for _d in range(2):
        for _k in range(SUBS):
            RECV["ag", _d, _s, _k] = RECV["rs", _d, _s, _k] = (_s * 2 + _d) * SUBS + _k
            SEND["ag", _d, _s, _k] = (_s % 2 * 2 + _d) * SUBS + _k
            SEND["rs", _d, _s, _k] = 4 * SUBS + (_s % 2 * 2 + _d) * SUBS + _k
_number(("og",), ("ogx", 0), ("ogx", 1), ("ogx", 2), *[("ogc", i) for i in range(4)])
_number(*[(n, r) for n in ("hid", "hg") for r in range(2)])
for _i in range(2):
    _number(("my", _i), *[("mx", j, _i) for j in range(3)], *[("mc", j, _i) for j in range(4)])


def body(
    gate, up, og, w, m1, m2, old_map, new_map,
    dg_out, du_out, nf_out, ns_out, sd_out,
    gate_v, up_v, fg, fu, m1_v, m2_v, old_v, new_v, og_s, og_v, hid, hgs, hgr, hg_own,
    wb, gb, rsb, mb, grad, dg_v, du_v, nf_v, ns_v, sd_v,
    ssem, rsem, lsem,
):
    dp, ow = lax.axis_index("dp"), lax.axis_index("owner")
    hi, z = dp // NZ, dp % NZ
    lo, x, core = ow // 8, (ow // 2) % NX, ow % 2
    y = hi * 2 + lo

    def dev(y_, x_, z_, c_):
        return ((y_ // 2) * NZ + z_, (y_ % 2) * 8 + x_ * 2 + c_)

    zn = (dev(y, x, (z + 1) % NZ, core), dev(y, x, (z + NZ - 1) % NZ, core))
    far = dev((y + 2) % NY, x, z, core)
    lows = dev((y // 2) * 2 + 1 - lo, x, z, core)
    xn = (dev(y, (x + 1) % NX, z, core), dev(y, (x + NX - 1) % NX, z, core))
    across = dev(y, (x + 2) % NX, z, core)
    cn = dev(y, x, z, 1 - core)
    other = dev((y + NY - 1 + 2 * lo) % NY, x, z, core)

    started = {}

    def copy(name, src, dst, device):
        return pltpu.make_async_remote_copy(
            src_ref=src, dst_ref=dst, send_sem=ssem.at[SEND[name]], recv_sem=rsem.at[RECV[name]],
            device_id=device, device_id_type=MESH,
        )

    def send(name, src, dst, device):
        i = SEND[name]
        if i in started:
            started[i].wait_send()
        started[i] = copy(name, src, dst, device)
        started[i].start()

    def arrived(name, dst, device):
        copy(name, dst, dst, device).wait_recv()

    def local(i, src, dst):
        return pltpu.make_async_copy(src, dst, lsem.at[i])

    def rows_of(t):
        return pl.ds(pl.multiple_of(t * ROWS, 16), ROWS)

    def sub(k):
        return pl.ds(k * SUB, SUB)

    mine_d = pl.ds(pl.multiple_of(hi * HALF, 128), HALF)
    other_d = pl.ds(pl.multiple_of((1 - hi) * HALF, 128), HALF)

    def unit(x_, c_):
        return pl.ds(pl.multiple_of((x_ * 2 + c_) * UNIT, 16), UNIT)

    barrier = pltpu.get_barrier_semaphore()
    for n in (*zn, *xn, cn, far, other, lows, across):
        pl.semaphore_signal(barrier, inc=1, device_id=n, device_id_type=MESH)

    loads_w = [local(i, w.at[i], wb.at[rows_of(z), pl.ds(i * SLAB, SLAB)]) for i in range(CAP)]
    load_gate, load_up = local(6, gate, gate_v), local(7, up, up_v)
    load_og = local(8, og.at[:, mine_d], og_v.at[pl.ds(0, TOK)])
    load_m = [local(9, m1, m1_v), local(10, m2, m2_v)]
    load_map = [local(16, old_map, old_v), local(17, new_map, new_v)]
    load_unit = local(18, og.at[unit(x, core), other_d], og_s)
    for c in [load_unit, *loads_w, load_gate, load_up, load_og, *load_m, *load_map]:
        c.start()

    pl.semaphore_wait(barrier, 9)

    def og_part(x_, c_):
        return og_v.at[pl.ds(pl.multiple_of(TOK + (x_ * 2 + c_) * UNIT, 16), UNIT)]

    load_unit.wait()
    send(("og",), og_s, og_part(x, core), other)

    def hops(d, k):
        return HOPS if d == k % 2 else HOPS - 1

    def ag_slot(d, s):
        return (z + NZ - s) % NZ if d == 0 else (z + s) % NZ

    def ag_tick(s):
        for k in range(SUBS):
            for d in range(2):
                if 0 < s <= hops(d, k):
                    dst = wb.at[rows_of(ag_slot(d, s)), sub(k)]
                    arrived(("ag", d, s - 1, k), dst, zn[d])
                if s < hops(d, k):
                    ref = wb.at[rows_of(ag_slot(d, s)), sub(k)]
                    send(("ag", d, s, k), ref, ref, zn[d])

    def rs_dest(d, s, k):
        n = hops(d, k)
        return (z + n - s) % NZ if d == 0 else (z + NZ - n + s) % NZ

    def rs_tick(s):
        for k in range(SUBS):
            for d in range(2):
                if s >= hops(d, k):
                    continue
                mine = gb.at[rows_of(rs_dest(d, s, k)), sub(k)]
                if s == 0:
                    src = mine
                else:
                    src = rsb.at[d, s - 1, :, sub(k)]
                    arrived(("rs", d, s - 1, k), src, zn[d])
                    src[...] = (src[...].astype(F32) + mine[...].astype(F32)).astype(BF)
                send(("rs", d, s, k), src, rsb.at[d, s, :, sub(k)], zn[d])

    for c in loads_w:
        c.wait()
    ag_tick(0)

    load_gate.wait()
    load_up.wait()
    step = 64

    def hidden_rows(first):
        for slot in range(CAP):

            @pl.loop(0, TOK // 2 // step)
            def _(i):
                r = pl.ds(pl.multiple_of(first + i * step, step), step)
                g = gate_v[slot, r, :].astype(F32)
                u = up_v[slot, r, :].astype(F32)
                sig = jax.nn.sigmoid(g)
                gs = g * sig
                hid[r, pl.ds(slot * SLAB, SLAB)] = (gs * u).astype(BF)
                fu[slot, r, :] = gs
                fg[slot, r, :] = u * sig * (1.0 + g * (1.0 - sig))

    def half(r):
        return pl.ds(r * (TOK // 2), TOK // 2)

    def partner(r):
        return pl.ds(TOK + r * (TOK // 2), TOK // 2)

    for r in range(2):
        hidden_rows(r * (TOK // 2))

    def og_to(name, x_, device):
        send(name, og_part(x_, core), og_part(x_, core), device)

    arrived(("og",), og_part(x, core), other)
    for j, device in enumerate((*xn, across)):
        og_to(("ogx", j), x, device)
    og_to(("ogc", 0), x, cn)
    for r in range(2):
        send(("hid", r), hid.at[half(r)], hid.at[partner(r)], far)

    ag_tick(1)
    ag_tick(2)
    ag_tick(3)

    x1, x2, x3 = (x + 1) % NX, (x + 2) % NX, (x + 3) % NX
    me = x * 2 + core

    def mom(x_, i):
        return mb.at[x_ * 2 + core, i]

    def mom_copies():
        copies = []
        for j, device in enumerate((*xn, across)):
            copies += [copy(("mx", j, i), mom(x, i), mom(x, i), device) for i in range(2)]
        return copies + [copy(("mc", 0, i), mom(x, i), mom(x, i), cn) for i in range(2)]

    mom_y = [copy(("my", i), mom(x, i), mom(x, i), lows) for i in range(2)]

    for c in (*load_m, *load_map):
        c.wait()

    @pl.when(lo == 0)
    def _():
        @pl.loop(0, CAP_OLD)
        def _(j):
            mb[me, 0, j] = m1_v[j].astype(BF)
            mb[me, 1, j] = m2_v[j].astype(BF)

        for c in mom_copies():
            c.start()

    for j, x_ in enumerate((x3, x1, x2)):
        arrived(("ogx", j), og_part(x_, core), xn[0])
        og_to(("ogc", j + 1), x_, cn)
    ag_tick(4)
    ag_tick(5)
    for r in range(2):
        arrived(("hid", r), hid.at[partner(r)], far)

    @pl.when(lo == 0)
    def _():
        for c in mom_y:
            c.start()

    for j, x_ in enumerate((x, x3, x1, x2)):
        arrived(("ogc", j), og_part(x_, 1 - core), cn)
    load_og.wait()

    def grad_block(i):
        part = lax.dot_general(
            og_v[:, pl.ds(i * GB, GB)], hid[...], (((0,), (0,)), ((), ())),
            preferred_element_type=F32,
        )
        gb[pl.ds(i * GB, GB), :] = part.astype(BF)

    grad_block(0)
    grad_block(1)
    ag_tick(6)
    grad_block(2)
    grad_block(3)
    grad_block(4)
    rs_tick(0)
    ag_tick(7)
    rs_tick(1)
    ag_tick(8)

    def hidden_grad(first, out):
        @pl.loop(0, 3)
        def _(j):
            cols = pl.ds(pl.multiple_of(j * 256, 256), 256)
            out[:, cols] = jnp.dot(
                og_v[pl.ds(first, TOK), :], wb[:, cols], preferred_element_type=F32
            ).astype(out.dtype)

    hidden_grad(TOK, hgs)
    for r in range(2):
        send(("hg", r), hgs.at[half(r)], hgr.at[half(r)], far)
    rs_tick(2)
    hidden_grad(0, hg_own)

    @pl.when(lo == 1)
    def _():
        for c in mom_y:
            c.wait_recv()
        for c in mom_copies():
            c.start()

    rs_tick(3)

    same = (N_SLAB, N_SLAB)
    lane, row = lax.broadcasted_iota(jnp.int32, same, 1), lax.broadcasted_iota(jnp.int32, same, 0)
    diagonal, earlier = lane == row, row < lane

    def owners_ranks(ref):
        across = jnp.broadcast_to(ref[...], same)
        down = jnp.sum(jnp.where(diagonal, across, 0), axis=1, keepdims=True)
        rank = jnp.sum(jnp.where((across == down) & earlier, 1, 0), axis=0, keepdims=True)
        return ref[...], rank

    old_own, old_rank = owners_ranks(old_v)
    new_own, new_rank = owners_ranks(new_v)
    slots = []
    for k in range(CAP):
        here = (new_own == ow) & (new_rank == k)
        slots.append(
            tuple(jnp.sum(jnp.where(here, v, 0)) for v in (old_own, old_rank, jnp.ones_like(old_own)))
        )

    rs_tick(4)
    rs_tick(5)
    for j, x_ in enumerate((x3, x1, x2)):
        if j == 2:
            rs_tick(6)
        for i in range(2):
            arrived(("mx", j, i), mom(x_, i), xn[0])
            send(("mc", j + 1, i), mom(x_, i), mom(x_, i), cn)

    for r in range(2):
        arrived(("hg", r), hgr.at[half(r)], far)
    for k in range(CAP):
        live = slots[k][2].astype(F32)

        @pl.loop(0, TOK // step)
        def _(i):
            r = pl.ds(pl.multiple_of(i * step, step), step)
            c = pl.ds(k * SLAB, SLAB)
            hg = (hg_own[r, c] + hgr[r, c].astype(F32)) * live
            dg_v[k, r, :] = (hg * fg[k, r, :]).astype(BF)
            du_v[k, r, :] = (hg * fu[k, r, :]).astype(BF)

    out_d = [local(11, dg_v, dg_out), local(12, du_v, du_out)]
    for c in out_d:
        c.start()

    rs_tick(7)

    for j, x_ in enumerate((x, x3, x1, x2)):
        for i in range(2):
            ref = mb.at[x_ * 2 + 1 - core, i]
            arrived(("mc", j, i), ref, cn)

    for k in range(SUBS):
        total = gb[rows_of(z), sub(k)].astype(F32)
        for d in range(2):
            last = hops(d, k) - 1
            ref = rsb.at[d, last, :, sub(k)]
            arrived(("rs", d, last, k), ref, zn[d])
            total += ref[...].astype(F32)
        grad[:, sub(k)] = total * (TOK * 32) ** (-0.5)

    for k in range(CAP):
        q, j, n = slots[k]
        live = n.astype(F32)
        g = grad[:, pl.ds(k * SLAB, SLAB)]
        m = (LR1 * mb[q, 0, j].astype(F32) + 0.1 * g) * live
        s = (LR2 * mb[q, 1, j].astype(F32) + 0.05 * g * g) * live
        nf_v[k] = m
        ns_v[k] = s
        sd_v[k] = m / (1.0 - LR1**20) / (jnp.sqrt(s / (1.0 - LR2**20)) + 1e-08)

    out_m = [local(13, nf_v, nf_out), local(14, ns_v, ns_out), local(15, sd_v, sd_out)]
    for c in out_m:
        c.start()

    @pl.when(lo == 0)
    def _():
        for c in mom_y:
            c.wait_send()

    for c in (*started.values(), *mom_copies()):
        c.wait_send()
    for c in (*out_d, *out_m):
        c.wait()


def write_out(*refs):
    src, dst, held, sem = refs[:5], refs[5:10], refs[10:15], refs[15]
    first = [pltpu.make_async_copy(src[i], held[i], sem.at[i]) for i in range(5)]
    second = [pltpu.make_async_copy(held[i], dst[i], sem.at[5 + i]) for i in range(5)]
    for c in first:
        c.start()
    for a, b in zip(first, second):
        a.wait()
        b.start()
    for c in second:
        c.wait()


def per_device(gate, up, og, w, m1, m2, old_map, new_map):
    hbm = pl.BlockSpec(memory_space=pl.ANY)
    act = (CAP, TOK, SLAB)
    state = (CAP, ROWS, SLAB)
    old = (CAP_OLD, ROWS, SLAB)
    V = pltpu.VMEM
    outs = pl.pallas_call(
        body,
        out_shape=[jax.ShapeDtypeStruct(act, BF)] * 2 + [jax.ShapeDtypeStruct(state, F32)] * 3,
        in_specs=[hbm] * 8,
        out_specs=[hbm] * 5,
        scratch_shapes=[
            V(act, BF), V(act, BF), V(act, F32), V(act, F32), V(old, F32), V(old, F32), V((1, N_SLAB), jnp.int32), V((1, N_SLAB), jnp.int32),
            V((UNIT, HALF), BF), V((2 * TOK, HALF), BF), V((2 * TOK, COLS), BF),
            V((TOK, COLS), BF), V((TOK, COLS), BF), V((TOK, COLS), F32),
            V((HALF, COLS), BF), V((HALF, COLS), BF), V((2, HOPS, ROWS, COLS), BF),
            V((8, 2, *old), BF), V((ROWS, COLS), F32),
            V(act, BF), V(act, BF), V(state, F32), V(state, F32), V(state, F32),
            pltpu.SemaphoreType.DMA((len(set(SEND.values())),)),
            pltpu.SemaphoreType.DMA((len(set(RECV.values())),)),
            pltpu.SemaphoreType.DMA((19,)),
        ],
        compiler_params=pltpu.CompilerParams(
            collective_id=0, has_side_effects=True, vmem_limit_bytes=56 << 20
        ),
        cost_estimate=pl.CostEstimate(flops=6 * 10**9, bytes_accessed=12 * 10**6, transcendentals=0),
        name="step",
    )(
        gate[:, 0].transpose(1, 0, 2),
        up[:, 0].transpose(1, 0, 2),
        og,
        w[0].transpose(1, 0, 2),
        m1[0].transpose(1, 0, 2),
        m2[0].transpose(1, 0, 2),
        old_map[None],
        new_map[None],
    )
    dg, du, nf, ns, sd = pl.pallas_call(
        write_out,
        out_shape=[jax.ShapeDtypeStruct(o.shape, o.dtype) for o in outs],
        in_specs=[hbm] * 5,
        out_specs=[hbm] * 5,
        scratch_shapes=[*[V(o.shape, o.dtype) for o in outs], pltpu.SemaphoreType.DMA((10,))],
        name="write_out",
    )(*outs)
    return (
        dg.transpose(1, 0, 2)[:, None],
        du.transpose(1, 0, 2)[:, None],
        nf.transpose(1, 0, 2)[None],
        ns.transpose(1, 0, 2)[None],
        sd.transpose(1, 0, 2)[None],
    )


def solution(mesh):
    act, state = P("dp", "owner", None, None), P("owner", "dp", None, None)
    return jax.shard_map(
        per_device,
        mesh=mesh,
        in_specs=(act, act, P("dp", None), state, state, state, P(), P()),
        out_specs=(act, act, state, state, state),
        check_vma=False,
    )
```

```python
import functools

import jax
import jax.numpy as jnp
from jax import lax
from jax.experimental import pallas as pl
from jax.experimental.pallas import tpu as pltpu
from jax.sharding import PartitionSpec as P

MESH = pl.DeviceIdType.MESH
BF, F32 = jnp.bfloat16, jnp.float32
NZ, NY, NX = 16, 4, 4
HOPS = 8
CAP, CAP_OLD, SLAB = 6, 9, 128
TOK, WIDTH = 384, 2560
HALF = WIDTH // 2
ROWS = WIDTH // 32
COLS = CAP * SLAB
SUBS = 3
SUB = COLS // SUBS
UNIT = TOK // 8
GB = 256
N_SLAB = 54
LR1, LR2 = 0.9, 0.95

RECV, SEND = {}, {}


def _number(*names):
    for n in names:
        RECV[n], SEND[n] = len(set(RECV.values())), len(set(SEND.values()))


for _s in range(HOPS):
    for _d in range(2):
        for _k in range(SUBS):
            RECV["ag", _d, _s, _k] = RECV["rs", _d, _s, _k] = (_s * 2 + _d) * SUBS + _k
            SEND["ag", _d, _s, _k] = (_s % 2 * 2 + _d) * SUBS + _k
            SEND["rs", _d, _s, _k] = 4 * SUBS + (_s % 2 * 2 + _d) * SUBS + _k
_number(("og",), ("ogx", 0), ("ogx", 1), ("ogx", 2), *[("ogc", i) for i in range(4)])
_number(*[(n, k) for n in ("hid", "hg") for k in range(SUBS)])
for _i in range(2):
    _number(("my", _i), *[("mx", j, _i) for j in range(3)], *[("mc", j, _i) for j in range(4)])


def body(
    gate, up, og, w, m1, m2, old_map, new_map,
    dg_v, du_v, nf_v, ns_v, sd_v,
    gate_v, up_v, fg, fu, m1_v, m2_v, old_v, new_v, og_s, og_v, ogt, hid, hgs, hgr, hg_own,
    wb, gb, rsb, mb, grad,
    ssem, rsem, lsem,
):
    dp, ow = lax.axis_index("dp"), lax.axis_index("owner")
    hi, z = dp // NZ, dp % NZ
    lo, x, core = ow // 8, (ow // 2) % NX, ow % 2
    y = hi * 2 + lo

    def dev(y_, x_, z_, c_):
        return ((y_ // 2) * NZ + z_, (y_ % 2) * 8 + x_ * 2 + c_)

    zn = (dev(y, x, (z + 1) % NZ, core), dev(y, x, (z + NZ - 1) % NZ, core))
    far = dev((y + 2) % NY, x, z, core)
    lows = dev((y // 2) * 2 + 1 - lo, x, z, core)
    xn = (dev(y, (x + 1) % NX, z, core), dev(y, (x + NX - 1) % NX, z, core))
    across = dev(y, (x + 2) % NX, z, core)
    cn = dev(y, x, z, 1 - core)
    other = dev((y + NY - 1 + 2 * lo) % NY, x, z, core)

    started = {}

    def copy(name, src, dst, device):
        return pltpu.make_async_remote_copy(
            src_ref=src, dst_ref=dst, send_sem=ssem.at[SEND[name]], recv_sem=rsem.at[RECV[name]],
            device_id=device, device_id_type=MESH,
        )

    def send(name, src, dst, device):
        i = SEND[name]
        if i in started:
            started[i].wait_send()
        started[i] = copy(name, src, dst, device)
        started[i].start()

    def arrived(name, dst, device):
        copy(name, dst, dst, device).wait_recv()

    def local(i, src, dst):
        return pltpu.make_async_copy(src, dst, lsem.at[i])

    def rows_of(t):
        return pl.ds(pl.multiple_of(t * ROWS, 16), ROWS)

    def sub(k):
        return pl.ds(k * SUB, SUB)

    mine_d = pl.ds(pl.multiple_of(hi * HALF, 128), HALF)
    other_d = pl.ds(pl.multiple_of((1 - hi) * HALF, 128), HALF)

    def unit(x_, c_):
        return pl.ds(pl.multiple_of((x_ * 2 + c_) * UNIT, 16), UNIT)

    barrier = pltpu.get_barrier_semaphore()
    for n in (*zn, *xn, cn, far, other, lows, across):
        pl.semaphore_signal(barrier, inc=1, device_id=n, device_id_type=MESH)

    loads_w = [local(i, w.at[i], wb.at[rows_of(z), pl.ds(i * SLAB, SLAB)]) for i in range(CAP)]
    load_gate, load_up = local(6, gate, gate_v), local(7, up, up_v)
    load_og = local(8, og.at[:, mine_d], og_v.at[pl.ds(0, TOK)])
    load_m = [local(9, m1, m1_v), local(10, m2, m2_v)]
    load_map = [local(16, old_map, old_v), local(17, new_map, new_v)]
    load_unit = local(18, og.at[unit(x, core), other_d], og_s)
    for c in [load_unit, *loads_w, load_gate, load_up, load_og, *load_m, *load_map]:
        c.start()

    pl.semaphore_wait(barrier, 9)

    def og_part(x_, c_):
        return og_v.at[pl.ds(pl.multiple_of(TOK + (x_ * 2 + c_) * UNIT, 16), UNIT)]

    load_unit.wait()
    send(("og",), og_s, og_part(x, core), other)

    def hops(d, k):
        return HOPS if d == k % 2 else HOPS - 1

    def ag_slot(d, s):
        return (z + NZ - s) % NZ if d == 0 else (z + s) % NZ

    def ag(s, *parts):
        for k in parts or range(SUBS):
            for d in range(2):
                if s > hops(d, k):
                    continue
                ref = wb.at[rows_of(ag_slot(d, s)), sub(k)]
                if s > 0:
                    arrived(("ag", d, s - 1, k), ref, zn[d])
                if s < hops(d, k):
                    send(("ag", d, s, k), ref, ref, zn[d])

    def rs_dest(d, s, k):
        n = hops(d, k)
        return (z + n - s) % NZ if d == 0 else (z + NZ - n + s) % NZ

    def rs(s, k):
        for d in range(2):
            n = hops(d, k)
            if s > n:
                continue
            if s == 0:
                src = gb.at[rows_of(rs_dest(d, s, k)), sub(k)]
            else:
                src = rsb.at[d, s - 1, :, sub(k)]
                arrived(("rs", d, s - 1, k), src, zn[d])
                if s == n:
                    continue
                mine = gb[rows_of(rs_dest(d, s, k)), sub(k)]
                src[...] = (src[...].astype(F32) + mine.astype(F32)).astype(BF)
            send(("rs", d, s, k), src, rsb.at[d, s, :, sub(k)], zn[d])

    def rs_sum(k):
        total = gb[rows_of(z), sub(k)].astype(F32)
        for d in range(2):
            total += rsb[d, hops(d, k) - 1, :, sub(k)].astype(F32)
        grad[:, sub(k)] = total * (TOK * 32) ** (-0.5)

    for c in loads_w:
        c.wait()
    ag(0, 0)

    load_gate.wait()
    load_up.wait()
    step = 64

    for slot in range(CAP):

        @pl.loop(0, TOK // step)
        def _(i):
            r = pl.ds(pl.multiple_of(i * step, step), step)
            g = gate_v[slot, r, :].astype(F32)
            u = up_v[slot, r, :].astype(F32)
            sig = jax.nn.sigmoid(g)
            gs = g * sig
            hid[r, pl.ds(slot * SLAB, SLAB)] = (gs * u).astype(BF)
            fu[slot, r, :] = gs
            fg[slot, r, :] = u * sig * (1.0 + g * (1.0 - sig))

    own, theirs = pl.ds(0, TOK), pl.ds(TOK, TOK)

    def hid_to(k):
        send(("hid", k), hid.at[own, sub(k)], hid.at[theirs, sub(k)], far)

    def turn(tokens):
        for i in range(HALF // GB):
            ogt[pl.ds(i * GB, GB), tokens] = og_v[tokens, pl.ds(i * GB, GB)].T

    ag(0, 1)
    load_og.wait()
    turn(own)

    x1, x2, x3 = (x + 1) % NX, (x + 2) % NX, (x + 3) % NX
    me = x * 2 + core

    def mom(x_, i):
        return mb.at[x_ * 2 + core, i]

    def mom_copies():
        copies = []
        for j, device in enumerate((*xn, across)):
            copies += [copy(("mx", j, i), mom(x, i), mom(x, i), device) for i in range(2)]
        return copies + [copy(("mc", 0, i), mom(x, i), mom(x, i), cn) for i in range(2)]

    mom_y = [copy(("my", i), mom(x, i), mom(x, i), lows) for i in range(2)]

    for c in (*load_m, *load_map):
        c.wait()

    @pl.when(lo == 0)
    def _():
        @pl.loop(0, CAP_OLD)
        def _(j):
            mb[me, 0, j] = m1_v[j].astype(BF)
            mb[me, 1, j] = m2_v[j].astype(BF)

    ag(0, 2)

    def og_to(name, x_, device):
        send(name, og_part(x_, core), og_part(x_, core), device)

    ag(1, 0)
    arrived(("og",), og_part(x, core), other)
    for j, device in enumerate((*xn, across)):
        og_to(("ogx", j), x, device)
    og_to(("ogc", 0), x, cn)
    hid_to(0)
    ag(1, 1, 2)
    ag(2)
    hid_to(1)
    ag(3, 0)
    for j, x_ in enumerate((x3, x1, x2)):
        arrived(("ogx", j), og_part(x_, core), xn[0])
        og_to(("ogc", j + 1), x_, cn)

    @pl.when(lo == 0)
    def _():
        for c in mom_copies():
            c.start()

    ag(3, 1, 2)
    hid_to(2)
    for j, x_ in enumerate((x, x3, x1, x2)):
        arrived(("ogc", j), og_part(x_, 1 - core), cn)
    turn(theirs)

    def gradient(k):
        arrived(("hid", k), hid.at[theirs, sub(k)], far)

        @pl.loop(0, 2)
        def _(i):
            r = pl.ds(pl.multiple_of(i * (HALF // 2), 128), HALF // 2)
            gb[r, sub(k)] = jnp.dot(
                ogt[r, :], hid[:, sub(k)], preferred_element_type=F32
            ).astype(BF)

    def mom_y_start(i):
        @pl.when(lo == 0)
        def _():
            mom_y[i].start()

    gradient(0)
    rs(0, 0)
    mom_y_start(0)
    ag(4)
    gradient(1)
    rs(1, 0)
    rs(0, 1)
    mom_y_start(1)
    ag(5)
    gradient(2)
    rs(2, 0)
    rs(1, 1)
    rs(0, 2)
    ag(6)
    rs(1, 2)
    rs(3, 0)
    ag(7)
    rs(2, 2)
    rs(2, 1)

    @pl.when(lo == 1)
    def _():
        for c in mom_y:
            c.wait_recv()
        for c in mom_copies():
            c.start()

    def hidden_grad(tokens, k, out):
        out[:, sub(k)] = jnp.dot(
            og_v[tokens, :], wb[:, sub(k)], preferred_element_type=F32
        ).astype(out.dtype)

    for k in range(SUBS):
        ag(8, k)
        hidden_grad(theirs, k, hgs)
        send(("hg", k), hgs.at[:, sub(k)], hgr.at[:, sub(k)], far)
    rs(3, 2)
    rs(3, 1)
    hidden_grad(own, 0, hg_own)

    same = (N_SLAB, N_SLAB)
    lane, row = lax.broadcasted_iota(jnp.int32, same, 1), lax.broadcasted_iota(jnp.int32, same, 0)
    diagonal, earlier = lane == row, row < lane

    def owners_ranks(ref):
        across = jnp.broadcast_to(ref[...], same)
        down = jnp.sum(jnp.where(diagonal, across, 0), axis=1, keepdims=True)
        rank = jnp.sum(jnp.where((across == down) & earlier, 1, 0), axis=0, keepdims=True)
        return ref[...], rank

    old_own, old_rank = owners_ranks(old_v)
    new_own, new_rank = owners_ranks(new_v)
    slots = []
    for k in range(CAP):
        here = (new_own == ow) & (new_rank == k)
        slots.append(
            tuple(jnp.sum(jnp.where(here, v, 0)) for v in (old_own, old_rank, jnp.ones_like(old_own)))
        )

    for k in range(SUBS):
        rs(4, k)
    hidden_grad(own, 1, hg_own)

    def mom_on(j, x_):
        for i in range(2):
            arrived(("mx", j, i), mom(x_, i), xn[0])
            send(("mc", j + 1, i), mom(x_, i), mom(x_, i), cn)

    for k in range(SUBS):
        rs(5, k)
    hidden_grad(own, 2, hg_own)
    mom_on(0, x3)
    mom_on(1, x1)

    def cotangents(part):
        arrived(("hg", part), hgr.at[:, sub(part)], far)
        for k in range(part * CAP // SUBS, (part + 1) * CAP // SUBS):
            live = slots[k][2].astype(F32)

            @pl.loop(0, TOK // step)
            def _(i):
                r = pl.ds(pl.multiple_of(i * step, step), step)
                c = pl.ds(k * SLAB, SLAB)
                hg = (hg_own[r, c] + hgr[r, c].astype(F32)) * live
                dg_v[k, r, :] = (hg * fg[k, r, :]).astype(BF)
                du_v[k, r, :] = (hg * fu[k, r, :]).astype(BF)

    for k in range(SUBS):
        rs(6, k)
    mom_on(2, x2)
    cotangents(0)
    for k in range(SUBS):
        rs(7, k)
    cotangents(1)
    cotangents(2)
    def adam(part):
        for k in range(part * CAP // SUBS, (part + 1) * CAP // SUBS):
            q, j, n = slots[k]
            live = n.astype(F32)
            g = grad[:, pl.ds(k * SLAB, SLAB)]
            m = (LR1 * mb[q, 0, j].astype(F32) + 0.1 * g) * live
            s = (LR2 * mb[q, 1, j].astype(F32) + 0.05 * g * g) * live
            nf_v[k] = m
            ns_v[k] = s
            sd_v[k] = m / (1.0 - LR1**20) / (jnp.sqrt(s / (1.0 - LR2**20)) + 1e-08)

    for j, x_ in enumerate((x, x3, x1, x2)):
        for i in range(2):
            ref = mb.at[x_ * 2 + 1 - core, i]
            arrived(("mc", j, i), ref, cn)
    for k in range(SUBS):
        rs(8, k)
        rs_sum(k)
        adam(k)

    @pl.when(lo == 0)
    def _():
        for c in mom_y:
            c.wait_send()

    for c in (*started.values(), *mom_copies()):
        c.wait_send()


def write_out(*refs):
    src, dst, sem = refs[:5], refs[5:10], refs[10]
    copies = [pltpu.make_async_copy(src[i], dst[i], sem.at[i]) for i in range(5)]
    for c in copies:
        c.start()
    for c in copies:
        c.wait()


def per_device(gate, up, og, w, m1, m2, old_map, new_map):
    hbm = pl.BlockSpec(memory_space=pl.ANY)
    act = (CAP, TOK, SLAB)
    state = (CAP, ROWS, SLAB)
    old = (CAP_OLD, ROWS, SLAB)
    V = pltpu.VMEM
    outs = pl.pallas_call(
        body,
        out_shape=[V(act, BF)] * 2 + [V(state, F32)] * 3,
        in_specs=[hbm] * 8,
        out_specs=[pl.BlockSpec(memory_space=V)] * 5,
        scratch_shapes=[
            V(act, BF), V(act, BF), V(act, F32), V(act, F32), V(old, F32), V(old, F32), V((1, N_SLAB), jnp.int32), V((1, N_SLAB), jnp.int32),
            V((UNIT, HALF), BF), V((2 * TOK, HALF), BF), V((HALF, 2 * TOK), BF), V((2 * TOK, COLS), BF),
            V((TOK, COLS), BF), V((TOK, COLS), BF), V((TOK, COLS), F32),
            V((HALF, COLS), BF), V((HALF, COLS), BF), V((2, HOPS, ROWS, COLS), BF),
            V((8, 2, *old), BF), V((ROWS, COLS), F32),
            pltpu.SemaphoreType.DMA((len(set(SEND.values())),)),
            pltpu.SemaphoreType.DMA((len(set(RECV.values())),)),
            pltpu.SemaphoreType.DMA((19,)),
        ],
        compiler_params=pltpu.CompilerParams(
            collective_id=0, has_side_effects=True, vmem_limit_bytes=40 << 20
        ),
        cost_estimate=pl.CostEstimate(flops=6 * 10**9, bytes_accessed=12 * 10**6, transcendentals=0),
        name="step",
    )(*[pltpu.with_memory_space_constraint(v, pltpu.HBM) for v in (
        gate[:, 0].transpose(1, 0, 2),
        up[:, 0].transpose(1, 0, 2),
        og,
        w[0].transpose(1, 0, 2),
        m1[0].transpose(1, 0, 2),
        m2[0].transpose(1, 0, 2),
        old_map[None],
        new_map[None],
    )])
    dg, du, nf, ns, sd = pl.pallas_call(
        write_out,
        out_shape=[jax.ShapeDtypeStruct(o.shape, o.dtype) for o in outs],
        in_specs=[pl.BlockSpec(memory_space=V)] * 5,
        out_specs=[hbm] * 5,
        scratch_shapes=[pltpu.SemaphoreType.DMA((5,))],
        name="write_out",
    )(*[pltpu.with_memory_space_constraint(o, V) for o in outs])
    return (
        dg.transpose(1, 0, 2)[:, None],
        du.transpose(1, 0, 2)[:, None],
        nf.transpose(1, 0, 2)[None],
        ns.transpose(1, 0, 2)[None],
        sd.transpose(1, 0, 2)[None],
    )


def solution(mesh):
    act, state = P("dp", "owner", None, None), P("owner", "dp", None, None)
    return jax.shard_map(
        per_device,
        mesh=mesh,
        in_specs=(act, act, P("dp", None), state, state, state, P(), P()),
        out_specs=(act, act, state, state, state),
        check_vma=False,
    )
```

```python
import functools

import jax
import jax.numpy as jnp
from jax import lax
from jax.experimental import pallas as pl
from jax.experimental.pallas import tpu as pltpu
from jax.sharding import PartitionSpec as P

MESH = pl.DeviceIdType.MESH
BF, F32 = jnp.bfloat16, jnp.float32
NZ, NY, NX = 16, 4, 4
HOPS = 8
CAP, CAP_OLD, SLAB = 6, 9, 128
TOK, WIDTH = 384, 2560
HALF = WIDTH // 2
ROWS = WIDTH // 32
COLS = CAP * SLAB
SUBS = 3
SUB = COLS // SUBS
UNIT = TOK // 8
GB = 256
N_SLAB = 54
LR1, LR2 = 0.9, 0.95

RECV, SEND = {}, {}


def _number(*names):
    for n in names:
        RECV[n], SEND[n] = len(set(RECV.values())), len(set(SEND.values()))


for _s in range(HOPS):
    for _d in range(2):
        for _k in range(SUBS):
            RECV["ag", _d, _s, _k] = RECV["rs", _d, _s, _k] = (_s * 2 + _d) * SUBS + _k
            SEND["ag", _d, _s, _k] = (_s % 2 * 2 + _d) * SUBS + _k
            SEND["rs", _d, _s, _k] = 4 * SUBS + (_s % 2 * 2 + _d) * SUBS + _k
_number(("og",), ("ogx", 0), ("ogx", 1), ("ogx", 2), *[("ogc", i) for i in range(4)])
_number(*[(n, k) for n in ("hid", "hg") for k in range(SUBS)])
for _i in range(2):
    _number(("my", _i), *[("mx", j, _i) for j in range(3)], *[("mc", j, _i) for j in range(4)])


def body(
    gate, up, og, w, m1, m2, old_map, new_map,
    dg_v, du_v, nf_v, ns_v, sd_v,
    gate_v, up_v, fg, fu, m1_v, m2_v, old_v, new_v, og_s, og_v, ogt, hid, hgs, hgr, hg_own,
    wb, gb, rsb, mb, grad,
    ssem, rsem, lsem,
):
    dp, ow = lax.axis_index("dp"), lax.axis_index("owner")
    hi, z = dp // NZ, dp % NZ
    lo, x, core = ow // 8, (ow // 2) % NX, ow % 2
    y = hi * 2 + lo

    def dev(y_, x_, z_, c_):
        return ((y_ // 2) * NZ + z_, (y_ % 2) * 8 + x_ * 2 + c_)

    zn = (dev(y, x, (z + 1) % NZ, core), dev(y, x, (z + NZ - 1) % NZ, core))
    far = dev((y + 2) % NY, x, z, core)
    lows = dev((y // 2) * 2 + 1 - lo, x, z, core)
    xn = (dev(y, (x + 1) % NX, z, core), dev(y, (x + NX - 1) % NX, z, core))
    across = dev(y, (x + 2) % NX, z, core)
    cn = dev(y, x, z, 1 - core)
    other = dev((y + NY - 1 + 2 * lo) % NY, x, z, core)

    started = {}

    def copy(name, src, dst, device):
        return pltpu.make_async_remote_copy(
            src_ref=src, dst_ref=dst, send_sem=ssem.at[SEND[name]], recv_sem=rsem.at[RECV[name]],
            device_id=device, device_id_type=MESH,
        )

    def send(name, src, dst, device):
        i = SEND[name]
        if i in started:
            started[i].wait_send()
        started[i] = copy(name, src, dst, device)
        started[i].start()

    def arrived(name, dst, device):
        copy(name, dst, dst, device).wait_recv()

    def local(i, src, dst):
        return pltpu.make_async_copy(src, dst, lsem.at[i])

    def rows_of(t):
        return pl.ds(pl.multiple_of(t * ROWS, 16), ROWS)

    def sub(k):
        return pl.ds(k * SUB, SUB)

    mine_d = pl.ds(pl.multiple_of(hi * HALF, 128), HALF)
    other_d = pl.ds(pl.multiple_of((1 - hi) * HALF, 128), HALF)

    def unit(x_, c_):
        return pl.ds(pl.multiple_of((x_ * 2 + c_) * UNIT, 16), UNIT)

    barrier = pltpu.get_barrier_semaphore()
    for n in (*zn, *xn, cn, far, other, lows, across):
        pl.semaphore_signal(barrier, inc=1, device_id=n, device_id_type=MESH)

    loads_w = [local(i, w.at[i], wb.at[rows_of(z), pl.ds(i * SLAB, SLAB)]) for i in range(CAP)]
    load_gate, load_up = local(6, gate, gate_v), local(7, up, up_v)
    load_og = local(8, og.at[:, mine_d], og_v.at[pl.ds(0, TOK)])
    load_m = [local(9, m1, m1_v), local(10, m2, m2_v)]
    load_map = [local(16, old_map, old_v), local(17, new_map, new_v)]
    load_unit = local(18, og.at[unit(x, core), other_d], og_s)
    for c in [load_unit, *loads_w, load_gate, load_up, load_og, *load_m, *load_map]:
        c.start()

    pl.semaphore_wait(barrier, 9)

    def og_part(x_, c_):
        return og_v.at[pl.ds(pl.multiple_of(TOK + (x_ * 2 + c_) * UNIT, 16), UNIT)]

    load_unit.wait()
    send(("og",), og_s, og_part(x, core), other)

    def hops(d, k):
        return HOPS if d == k % 2 else HOPS - 1

    def ag_slot(d, s):
        return (z + NZ - s) % NZ if d == 0 else (z + s) % NZ

    def ag(s, *parts):
        for k in parts or range(SUBS):
            for d in range(2):
                if s > hops(d, k):
                    continue
                ref = wb.at[rows_of(ag_slot(d, s)), sub(k)]
                if s > 0:
                    arrived(("ag", d, s - 1, k), ref, zn[d])
                if s < hops(d, k):
                    send(("ag", d, s, k), ref, ref, zn[d])

    def rs_dest(d, s, k):
        n = hops(d, k)
        return (z + n - s) % NZ if d == 0 else (z + NZ - n + s) % NZ

    def rs(s, k):
        for d in range(2):
            n = hops(d, k)
            if s > n:
                continue
            if s == 0:
                src = gb.at[rows_of(rs_dest(d, s, k)), sub(k)]
            else:
                src = rsb.at[d, s - 1, :, sub(k)]
                arrived(("rs", d, s - 1, k), src, zn[d])
                if s == n:
                    continue
                mine = gb[rows_of(rs_dest(d, s, k)), sub(k)]
                src[...] = (src[...].astype(F32) + mine.astype(F32)).astype(BF)
            send(("rs", d, s, k), src, rsb.at[d, s, :, sub(k)], zn[d])

    def rs_sum(k):
        total = gb[rows_of(z), sub(k)].astype(F32)
        for d in range(2):
            total += rsb[d, hops(d, k) - 1, :, sub(k)].astype(F32)
        grad[:, sub(k)] = total * (TOK * 32) ** (-0.5)

    for c in loads_w:
        c.wait()
    ag(0, 0)

    load_gate.wait()
    load_up.wait()
    step = 64

    for slot in range(CAP):

        @pl.loop(0, TOK // step)
        def _(i):
            r = pl.ds(pl.multiple_of(i * step, step), step)
            g = gate_v[slot, r, :].astype(F32)
            u = up_v[slot, r, :].astype(F32)
            sig = jax.nn.sigmoid(g)
            gs = g * sig
            hid[r, pl.ds(slot * SLAB, SLAB)] = (gs * u).astype(BF)
            fu[slot, r, :] = gs
            fg[slot, r, :] = u * sig * (1.0 + g * (1.0 - sig))

    own, theirs = pl.ds(0, TOK), pl.ds(TOK, TOK)

    def hid_to(k):
        send(("hid", k), hid.at[own, sub(k)], hid.at[theirs, sub(k)], far)

    def turn(tokens):
        for i in range(HALF // GB):
            ogt[pl.ds(i * GB, GB), tokens] = og_v[tokens, pl.ds(i * GB, GB)].T

    ag(0, 1)
    load_og.wait()
    turn(own)

    x1, x2, x3 = (x + 1) % NX, (x + 2) % NX, (x + 3) % NX
    me = x * 2 + core

    def mom(x_, i):
        return mb.at[x_ * 2 + core, i]

    def mom_copies(i):
        targets = [(("mx", j, i), device) for j, device in enumerate((*xn, across))]
        return [copy(n, mom(x, i), mom(x, i), device) for n, device in (*targets, (("mc", 0, i), cn))]

    mom_y = [copy(("my", i), mom(x, i), mom(x, i), lows) for i in range(2)]

    for c in (*load_m, *load_map):
        c.wait()

    @pl.when(lo == 0)
    def _():
        @pl.loop(0, CAP_OLD)
        def _(j):
            mb[me, 0, j] = m1_v[j].astype(BF)
            mb[me, 1, j] = m2_v[j].astype(BF)

    ag(0, 2)

    def og_to(name, x_, device):
        send(name, og_part(x_, core), og_part(x_, core), device)

    ag(1, 0)
    arrived(("og",), og_part(x, core), other)
    for j, device in enumerate((*xn, across)):
        og_to(("ogx", j), x, device)
    og_to(("ogc", 0), x, cn)
    hid_to(0)
    ag(1, 1, 2)
    ag(2)
    hid_to(1)
    ag(3, 0)
    for j, x_ in enumerate((x3, x1, x2)):
        arrived(("ogx", j), og_part(x_, core), xn[0])
        og_to(("ogc", j + 1), x_, cn)

    @pl.when(lo == 0)
    def _():
        for c in (*mom_copies(0), *mom_copies(1)):
            c.start()

    ag(3, 1, 2)
    hid_to(2)
    for j, x_ in enumerate((x, x3, x1, x2)):
        arrived(("ogc", j), og_part(x_, 1 - core), cn)
    turn(theirs)

    def gradient(k):
        arrived(("hid", k), hid.at[theirs, sub(k)], far)

        @pl.loop(0, 2)
        def _(i):
            r = pl.ds(pl.multiple_of(i * (HALF // 2), 128), HALF // 2)
            gb[r, sub(k)] = jnp.dot(
                ogt[r, :], hid[:, sub(k)], preferred_element_type=F32
            ).astype(BF)

    def mom_y_start(i):
        @pl.when(lo == 0)
        def _():
            mom_y[i].start()

    gradient(0)
    rs(0, 0)
    mom_y_start(0)
    ag(4)
    gradient(1)
    rs(1, 0)
    rs(0, 1)
    mom_y_start(1)
    ag(5)
    gradient(2)
    rs(2, 0)
    rs(1, 1)
    rs(0, 2)
    def mom_round(i):
        @pl.when(lo == 1)
        def _():
            mom_y[i].wait_recv()
            for c in mom_copies(i):
                c.start()

    ag(6)
    mom_round(0)
    rs(1, 2)
    mom_round(1)
    ag(7, 0, 1)
    rs(2, 2)
    rs(2, 1)

    def hidden_grad(tokens, k, out):
        out[:, sub(k)] = jnp.dot(
            og_v[tokens, :], wb[:, sub(k)], preferred_element_type=F32
        ).astype(out.dtype)

    def hg_to(k):
        hidden_grad(theirs, k, hgs)
        send(("hg", k), hgs.at[:, sub(k)], hgr.at[:, sub(k)], far)

    rs(3, 0)
    ag(8, 0, 1)
    for k in (2, 1):
        rs(3, k)
    hg_to(0)
    hg_to(1)
    ag(7, 2)
    for k in (2, 1, 0):
        rs(4, k)
    hidden_grad(own, 0, hg_own)

    same = (N_SLAB, N_SLAB)
    lane, row = lax.broadcasted_iota(jnp.int32, same, 1), lax.broadcasted_iota(jnp.int32, same, 0)
    diagonal, earlier = lane == row, row < lane

    def owners_ranks(ref):
        across = jnp.broadcast_to(ref[...], same)
        down = jnp.sum(jnp.where(diagonal, across, 0), axis=1, keepdims=True)
        rank = jnp.sum(jnp.where((across == down) & earlier, 1, 0), axis=0, keepdims=True)
        return ref[...], rank

    old_own, old_rank = owners_ranks(old_v)
    new_own, new_rank = owners_ranks(new_v)
    slots = []
    for k in range(CAP):
        here = (new_own == ow) & (new_rank == k)
        slots.append(
            tuple(jnp.sum(jnp.where(here, v, 0)) for v in (old_own, old_rank, jnp.ones_like(old_own)))
        )

    ag(8, 2)
    for k in (2, 1, 0):
        rs(5, k)
    hg_to(2)
    hidden_grad(own, 1, hg_own)

    def mom_on(j, x_):
        for i in range(2):
            arrived(("mx", j, i), mom(x_, i), xn[0])
            send(("mc", j + 1, i), mom(x_, i), mom(x_, i), cn)

    mom_on(0, x3)
    mom_on(1, x1)

    def cotangents(part):
        arrived(("hg", part), hgr.at[:, sub(part)], far)
        for k in range(part * CAP // SUBS, (part + 1) * CAP // SUBS):
            live = slots[k][2].astype(F32)

            @pl.loop(0, TOK // step)
            def _(i):
                r = pl.ds(pl.multiple_of(i * step, step), step)
                c = pl.ds(k * SLAB, SLAB)
                hg = (hg_own[r, c] + hgr[r, c].astype(F32)) * live
                dg_v[k, r, :] = (hg * fg[k, r, :]).astype(BF)
                du_v[k, r, :] = (hg * fu[k, r, :]).astype(BF)

    for k in (2, 1, 0):
        rs(6, k)
    hidden_grad(own, 2, hg_own)
    mom_on(2, x2)
    cotangents(0)
    for k in (2, 1, 0):
        rs(7, k)
    cotangents(1)
    cotangents(2)
    def adam(part):
        for k in range(part * CAP // SUBS, (part + 1) * CAP // SUBS):
            q, j, n = slots[k]
            live = n.astype(F32)
            g = grad[:, pl.ds(k * SLAB, SLAB)]
            m = (LR1 * mb[q, 0, j].astype(F32) + 0.1 * g) * live
            s = (LR2 * mb[q, 1, j].astype(F32) + 0.05 * g * g) * live
            nf_v[k] = m
            ns_v[k] = s
            sd_v[k] = m / (1.0 - LR1**20) / (jnp.sqrt(s / (1.0 - LR2**20)) + 1e-08)

    for j, x_ in enumerate((x, x3, x1, x2)):
        for i in range(2):
            ref = mb.at[x_ * 2 + 1 - core, i]
            arrived(("mc", j, i), ref, cn)
    for k in (2, 1, 0):
        rs(8, k)
        rs_sum(k)
        adam(k)

    @pl.when(lo == 0)
    def _():
        for c in mom_y:
            c.wait_send()

    for c in (*started.values(), *mom_copies(0), *mom_copies(1)):
        c.wait_send()


def write_out(*refs):
    src, dst, sem = refs[:5], refs[5:10], refs[10]
    copies = [pltpu.make_async_copy(src[i], dst[i], sem.at[i]) for i in range(5)]
    for c in copies:
        c.start()
    for c in copies:
        c.wait()


def per_device(gate, up, og, w, m1, m2, old_map, new_map):
    hbm = pl.BlockSpec(memory_space=pl.ANY)
    act = (CAP, TOK, SLAB)
    state = (CAP, ROWS, SLAB)
    old = (CAP_OLD, ROWS, SLAB)
    V = pltpu.VMEM
    outs = pl.pallas_call(
        body,
        out_shape=[V(act, BF)] * 2 + [V(state, F32)] * 3,
        in_specs=[hbm] * 8,
        out_specs=[pl.BlockSpec(memory_space=V)] * 5,
        scratch_shapes=[
            V(act, BF), V(act, BF), V(act, F32), V(act, F32), V(old, F32), V(old, F32), V((1, N_SLAB), jnp.int32), V((1, N_SLAB), jnp.int32),
            V((UNIT, HALF), BF), V((2 * TOK, HALF), BF), V((HALF, 2 * TOK), BF), V((2 * TOK, COLS), BF),
            V((TOK, COLS), BF), V((TOK, COLS), BF), V((TOK, COLS), F32),
            V((HALF, COLS), BF), V((HALF, COLS), BF), V((2, HOPS, ROWS, COLS), BF),
            V((8, 2, *old), BF), V((ROWS, COLS), F32),
            pltpu.SemaphoreType.DMA((len(set(SEND.values())),)),
            pltpu.SemaphoreType.DMA((len(set(RECV.values())),)),
            pltpu.SemaphoreType.DMA((19,)),
        ],
        compiler_params=pltpu.CompilerParams(
            collective_id=0, has_side_effects=True, vmem_limit_bytes=40 << 20
        ),
        cost_estimate=pl.CostEstimate(flops=6 * 10**9, bytes_accessed=12 * 10**6, transcendentals=0),
        name="step",
    )(*[pltpu.with_memory_space_constraint(v, pltpu.HBM) for v in (
        gate[:, 0].transpose(1, 0, 2),
        up[:, 0].transpose(1, 0, 2),
        og,
        w[0].transpose(1, 0, 2),
        m1[0].transpose(1, 0, 2),
        m2[0].transpose(1, 0, 2),
        old_map[None],
        new_map[None],
    )])
    dg, du, nf, ns, sd = pl.pallas_call(
        write_out,
        out_shape=[jax.ShapeDtypeStruct(o.shape, o.dtype) for o in outs],
        in_specs=[pl.BlockSpec(memory_space=V)] * 5,
        out_specs=[hbm] * 5,
        scratch_shapes=[pltpu.SemaphoreType.DMA((5,))],
        name="write_out",
    )(*[pltpu.with_memory_space_constraint(o, V) for o in outs])
    return (
        dg.transpose(1, 0, 2)[:, None],
        du.transpose(1, 0, 2)[:, None],
        nf.transpose(1, 0, 2)[None],
        ns.transpose(1, 0, 2)[None],
        sd.transpose(1, 0, 2)[None],
    )


def solution(mesh):
    act, state = P("dp", "owner", None, None), P("owner", "dp", None, None)
    return jax.shard_map(
        per_device,
        mesh=mesh,
        in_specs=(act, act, P("dp", None), state, state, state, P(), P()),
        out_specs=(act, act, state, state, state),
        check_vma=False,
    )
```

```python
import functools

import jax
import jax.numpy as jnp
from jax import lax
from jax.experimental import pallas as pl
from jax.experimental.pallas import tpu as pltpu
from jax.sharding import PartitionSpec as P

MESH = pl.DeviceIdType.MESH
BF, F32 = jnp.bfloat16, jnp.float32
NZ, NY, NX = 16, 4, 4
HOPS = 8
CAP, CAP_OLD, SLAB = 6, 9, 128
TOK, WIDTH = 384, 2560
HALF = WIDTH // 2
ROWS = WIDTH // 32
COLS = CAP * SLAB
SUBS = 3
SUB = COLS // SUBS
UNIT = TOK // 8
GB = 256
N_SLAB = 54
LR1, LR2 = 0.9, 0.95

RECV, SEND = {}, {}


def _number(*names):
    for n in names:
        RECV[n], SEND[n] = len(set(RECV.values())), len(set(SEND.values()))


for _s in range(HOPS):
    for _d in range(2):
        for _k in range(SUBS):
            RECV["ag", _d, _s, _k] = RECV["rs", _d, _s, _k] = (_s * 2 + _d) * SUBS + _k
            SEND["ag", _d, _s, _k] = (_s % 2 * 2 + _d) * SUBS + _k
            SEND["rs", _d, _s, _k] = 4 * SUBS + (_s % 2 * 2 + _d) * SUBS + _k
_number(("og",), ("ogx", 0), ("ogx", 1), ("ogx", 2), *[("ogc", i) for i in range(4)])
_number(*[(n, k) for n in ("hid", "hg") for k in range(SUBS)])
for _i in range(2):
    _number(("my", _i), *[("mx", j, _i) for j in range(3)], *[("mc", j, _i) for j in range(4)])


def body(
    gate, up, og, w, m1, m2, old_map, new_map,
    dg_v, du_v, nf_v, ns_v, sd_v,
    gate_v, up_v, fg, fu, m1_v, m2_v, old_v, new_v, og_s, og_v, ogt, hid, hgs, hgr, hg_own,
    wb, gb, rsb, mb, grad,
    ssem, rsem, lsem,
):
    dp, ow = lax.axis_index("dp"), lax.axis_index("owner")
    hi, z = dp // NZ, dp % NZ
    lo, x, core = ow // 8, (ow // 2) % NX, ow % 2
    y = hi * 2 + lo

    def dev(y_, x_, z_, c_):
        return ((y_ // 2) * NZ + z_, (y_ % 2) * 8 + x_ * 2 + c_)

    zn = (dev(y, x, (z + 1) % NZ, core), dev(y, x, (z + NZ - 1) % NZ, core))
    far = dev((y + 2) % NY, x, z, core)
    lows = dev((y // 2) * 2 + 1 - lo, x, z, core)
    xn = (dev(y, (x + 1) % NX, z, core), dev(y, (x + NX - 1) % NX, z, core))
    across = dev(y, (x + 2) % NX, z, core)
    cn = dev(y, x, z, 1 - core)
    other = dev((y + NY - 1 + 2 * lo) % NY, x, z, core)

    started = {}

    def copy(name, src, dst, device):
        return pltpu.make_async_remote_copy(
            src_ref=src, dst_ref=dst, send_sem=ssem.at[SEND[name]], recv_sem=rsem.at[RECV[name]],
            device_id=device, device_id_type=MESH,
        )

    def send(name, src, dst, device):
        i = SEND[name]
        if i in started:
            started[i].wait_send()
        started[i] = copy(name, src, dst, device)
        started[i].start()

    def arrived(name, dst, device):
        copy(name, dst, dst, device).wait_recv()

    def local(i, src, dst):
        return pltpu.make_async_copy(src, dst, lsem.at[i])

    def rows_of(t):
        return pl.ds(pl.multiple_of(t * ROWS, 16), ROWS)

    def sub(k):
        return pl.ds(k * SUB, SUB)

    mine_d = pl.ds(pl.multiple_of(hi * HALF, 128), HALF)
    other_d = pl.ds(pl.multiple_of((1 - hi) * HALF, 128), HALF)

    def unit(x_, c_):
        return pl.ds(pl.multiple_of((x_ * 2 + c_) * UNIT, 16), UNIT)

    barrier = pltpu.get_barrier_semaphore()
    for n in (*zn, *xn, cn, far, other, lows, across):
        pl.semaphore_signal(barrier, inc=1, device_id=n, device_id_type=MESH)

    loads_w = [local(i, w.at[i], wb.at[rows_of(z), pl.ds(i * SLAB, SLAB)]) for i in range(CAP)]
    load_gate, load_up = local(6, gate, gate_v), local(7, up, up_v)
    load_og = local(8, og.at[:, mine_d], og_v.at[pl.ds(0, TOK)])
    load_m = [local(9, m1, m1_v), local(10, m2, m2_v)]
    load_map = [local(16, old_map, old_v), local(17, new_map, new_v)]
    load_unit = local(18, og.at[unit(x, core), other_d], og_s)
    for c in [load_unit, *loads_w, load_gate, load_up, load_og, *load_m, *load_map]:
        c.start()

    pl.semaphore_wait(barrier, 9)

    def og_part(x_, c_):
        return og_v.at[pl.ds(pl.multiple_of(TOK + (x_ * 2 + c_) * UNIT, 16), UNIT)]

    load_unit.wait()
    send(("og",), og_s, og_part(x, core), other)

    def hops(d, k):
        return HOPS if d == k % 2 else HOPS - 1

    def ag_slot(d, s):
        return (z + NZ - s) % NZ if d == 0 else (z + s) % NZ

    def ag(s, *parts):
        for k in parts or range(SUBS):
            for d in range(2):
                if s > hops(d, k):
                    continue
                ref = wb.at[rows_of(ag_slot(d, s)), sub(k)]
                if s > 0:
                    arrived(("ag", d, s - 1, k), ref, zn[d])
                if s < hops(d, k):
                    send(("ag", d, s, k), ref, ref, zn[d])

    def rs_dest(d, s, k):
        n = hops(d, k)
        return (z + n - s) % NZ if d == 0 else (z + NZ - n + s) % NZ

    def rs(s, k):
        for d in range(2):
            n = hops(d, k)
            if s > n:
                continue
            if s == 0:
                src = gb.at[rows_of(rs_dest(d, s, k)), sub(k)]
            else:
                src = rsb.at[d, s - 1, :, sub(k)]
                arrived(("rs", d, s - 1, k), src, zn[d])
                if s == n:
                    continue
                mine = gb[rows_of(rs_dest(d, s, k)), sub(k)]
                src[...] = (src[...].astype(F32) + mine.astype(F32)).astype(BF)
            send(("rs", d, s, k), src, rsb.at[d, s, :, sub(k)], zn[d])

    def rs_sum(k):
        total = gb[rows_of(z), sub(k)].astype(F32)
        for d in range(2):
            total += rsb[d, hops(d, k) - 1, :, sub(k)].astype(F32)
        grad[:, sub(k)] = total * (TOK * 32) ** (-0.5)

    for c in loads_w:
        c.wait()
    ag(0, 0)

    load_gate.wait()
    load_up.wait()
    step = 64

    for slot in range(CAP):

        @pl.loop(0, TOK // step)
        def _(i):
            r = pl.ds(pl.multiple_of(i * step, step), step)
            g = gate_v[slot, r, :].astype(F32)
            u = up_v[slot, r, :].astype(F32)
            sig = jax.nn.sigmoid(g)
            gs = g * sig
            hid[r, pl.ds(slot * SLAB, SLAB)] = (gs * u).astype(BF)
            fu[slot, r, :] = gs
            fg[slot, r, :] = u * sig * (1.0 + g * (1.0 - sig))

    own, theirs = pl.ds(0, TOK), pl.ds(TOK, TOK)

    def hid_to(k, c):
        name = ("hid", k)
        started[SEND[name]] = copy(name, hid.at[own, sub(k)], hid.at[theirs, sub(k)], far)

        @pl.when(core == c)
        def _():
            started[SEND[name]].start()

    def turn(tokens):
        for i in range(HALF // GB):
            ogt[pl.ds(i * GB, GB), tokens] = og_v[tokens, pl.ds(i * GB, GB)].T

    ag(0, 1)
    load_og.wait()
    turn(own)

    x1, x2, x3 = (x + 1) % NX, (x + 2) % NX, (x + 3) % NX
    me = x * 2 + core

    def mom(x_, i):
        return mb.at[x_ * 2 + core, i]

    def mom_copies(i):
        targets = [(("mx", j, i), device) for j, device in enumerate((*xn, across))]
        return [copy(n, mom(x, i), mom(x, i), device) for n, device in (*targets, (("mc", 0, i), cn))]

    mom_y = [copy(("my", i), mom(x, i), mom(x, i), lows) for i in range(2)]

    for c in (*load_m, *load_map):
        c.wait()

    @pl.when(lo == 0)
    def _():
        @pl.loop(0, CAP_OLD)
        def _(j):
            mb[me, 0, j] = m1_v[j].astype(BF)
            mb[me, 1, j] = m2_v[j].astype(BF)

    ag(0, 2)

    def og_to(name, x_, device):
        send(name, og_part(x_, core), og_part(x_, core), device)

    ag(1, 0)
    arrived(("og",), og_part(x, core), other)
    for j, device in enumerate((*xn, across)):
        og_to(("ogx", j), x, device)
    og_to(("ogc", 0), x, cn)
    hid_to(0, 0)
    ag(1, 1, 2)
    hid_to(1, 0)
    hid_to(0, 1)
    ag(2)
    hid_to(2, 0)
    hid_to(1, 1)
    ag(3, 0)
    for j, x_ in enumerate((x3, x1, x2)):
        arrived(("ogx", j), og_part(x_, core), xn[0])
        og_to(("ogc", j + 1), x_, cn)

    @pl.when(lo == 0)
    def _():
        for c in (*mom_copies(0), *mom_copies(1)):
            c.start()

    ag(3, 1, 2)
    hid_to(2, 1)
    for j, x_ in enumerate((x, x3, x1, x2)):
        arrived(("ogc", j), og_part(x_, 1 - core), cn)
    turn(theirs)

    def gradient(k):
        arrived(("hid", k), hid.at[theirs, sub(k)], far)

        @pl.loop(0, 2)
        def _(i):
            r = pl.ds(pl.multiple_of(i * (HALF // 2), 128), HALF // 2)
            gb[r, sub(k)] = jnp.dot(
                ogt[r, :], hid[:, sub(k)], preferred_element_type=F32
            ).astype(BF)

    def mom_y_start(i):
        @pl.when(lo == 0)
        def _():
            mom_y[i].start()

    gradient(0)
    rs(0, 0)
    mom_y_start(0)
    ag(4)
    gradient(1)
    rs(1, 0)
    rs(0, 1)
    mom_y_start(1)
    ag(5)
    gradient(2)
    rs(2, 0)
    rs(1, 1)
    rs(0, 2)
    def mom_round(i):
        @pl.when(lo == 1)
        def _():
            mom_y[i].wait_recv()
            for c in mom_copies(i):
                c.start()

    ag(6)
    mom_round(0)
    rs(1, 2)
    mom_round(1)
    ag(7, 0, 1)
    rs(2, 2)
    rs(2, 1)

    def hidden_grad(tokens, k, out):
        out[:, sub(k)] = jnp.dot(
            og_v[tokens, :], wb[:, sub(k)], preferred_element_type=F32
        ).astype(out.dtype)

    def hg_to(k):
        hidden_grad(theirs, k, hgs)
        send(("hg", k), hgs.at[:, sub(k)], hgr.at[:, sub(k)], far)

    rs(3, 0)
    ag(8, 0, 1)
    for k in (2, 1):
        rs(3, k)
    hg_to(0)
    ag(7, 2)
    for k in (2, 1, 0):
        rs(4, k)
    hg_to(1)

    same = (N_SLAB, N_SLAB)
    lane, row = lax.broadcasted_iota(jnp.int32, same, 1), lax.broadcasted_iota(jnp.int32, same, 0)
    diagonal, earlier = lane == row, row < lane

    def owners_ranks(ref):
        across = jnp.broadcast_to(ref[...], same)
        down = jnp.sum(jnp.where(diagonal, across, 0), axis=1, keepdims=True)
        rank = jnp.sum(jnp.where((across == down) & earlier, 1, 0), axis=0, keepdims=True)
        return ref[...], rank

    old_own, old_rank = owners_ranks(old_v)
    new_own, new_rank = owners_ranks(new_v)
    slots = []
    for k in range(CAP):
        here = (new_own == ow) & (new_rank == k)
        slots.append(
            tuple(jnp.sum(jnp.where(here, v, 0)) for v in (old_own, old_rank, jnp.ones_like(old_own)))
        )

    ag(8, 2)
    for k in (2, 1, 0):
        rs(5, k)
    hg_to(2)

    def mom_on(j, x_):
        for i in range(2):
            arrived(("mx", j, i), mom(x_, i), xn[0])
            send(("mc", j + 1, i), mom(x_, i), mom(x_, i), cn)

    mom_on(0, x3)
    mom_on(1, x1)

    def cotangents(part):
        arrived(("hg", part), hgr.at[:, sub(part)], far)
        for k in range(part * CAP // SUBS, (part + 1) * CAP // SUBS):
            live = slots[k][2].astype(F32)

            @pl.loop(0, TOK // step)
            def _(i):
                r = pl.ds(pl.multiple_of(i * step, step), step)
                c = pl.ds(k * SLAB, SLAB)
                hg = (hg_own[r, c] + hgr[r, c].astype(F32)) * live
                dg_v[k, r, :] = (hg * fg[k, r, :]).astype(BF)
                du_v[k, r, :] = (hg * fu[k, r, :]).astype(BF)

    for k in (2, 1, 0):
        rs(6, k)
    hidden_grad(own, 0, hg_own)
    mom_on(2, x2)
    cotangents(0)
    for k in (2, 1, 0):
        rs(7, k)
    for k in (1, 2):
        hidden_grad(own, k, hg_own)
        cotangents(k)
    def adam(part):
        for k in range(part * CAP // SUBS, (part + 1) * CAP // SUBS):
            q, j, n = slots[k]
            live = n.astype(F32)
            g = grad[:, pl.ds(k * SLAB, SLAB)]
            m = (LR1 * mb[q, 0, j].astype(F32) + 0.1 * g) * live
            s = (LR2 * mb[q, 1, j].astype(F32) + 0.05 * g * g) * live
            nf_v[k] = m
            ns_v[k] = s
            sd_v[k] = m / (1.0 - LR1**20) / (jnp.sqrt(s / (1.0 - LR2**20)) + 1e-08)

    for j, x_ in enumerate((x, x3, x1, x2)):
        for i in range(2):
            ref = mb.at[x_ * 2 + 1 - core, i]
            arrived(("mc", j, i), ref, cn)
    for k in (2, 1, 0):
        rs(8, k)
        rs_sum(k)
        adam(k)

    @pl.when(lo == 0)
    def _():
        for c in mom_y:
            c.wait_send()

    for c in (*started.values(), *mom_copies(0), *mom_copies(1)):
        c.wait_send()


def write_out(*refs):
    src, dst, sem = refs[:5], refs[5:10], refs[10]
    copies = [pltpu.make_async_copy(src[i], dst[i], sem.at[i]) for i in range(5)]
    for c in copies:
        c.start()
    for c in copies:
        c.wait()


def per_device(gate, up, og, w, m1, m2, old_map, new_map):
    hbm = pl.BlockSpec(memory_space=pl.ANY)
    act = (CAP, TOK, SLAB)
    state = (CAP, ROWS, SLAB)
    old = (CAP_OLD, ROWS, SLAB)
    V = pltpu.VMEM
    outs = pl.pallas_call(
        body,
        out_shape=[V(act, BF)] * 2 + [V(state, F32)] * 3,
        in_specs=[hbm] * 8,
        out_specs=[pl.BlockSpec(memory_space=V)] * 5,
        scratch_shapes=[
            V(act, BF), V(act, BF), V(act, F32), V(act, F32), V(old, F32), V(old, F32), V((1, N_SLAB), jnp.int32), V((1, N_SLAB), jnp.int32),
            V((UNIT, HALF), BF), V((2 * TOK, HALF), BF), V((HALF, 2 * TOK), BF), V((2 * TOK, COLS), BF),
            V((TOK, COLS), BF), V((TOK, COLS), BF), V((TOK, COLS), F32),
            V((HALF, COLS), BF), V((HALF, COLS), BF), V((2, HOPS, ROWS, COLS), BF),
            V((8, 2, *old), BF), V((ROWS, COLS), F32),
            pltpu.SemaphoreType.DMA((len(set(SEND.values())),)),
            pltpu.SemaphoreType.DMA((len(set(RECV.values())),)),
            pltpu.SemaphoreType.DMA((19,)),
        ],
        compiler_params=pltpu.CompilerParams(
            collective_id=0, has_side_effects=True, vmem_limit_bytes=40 << 20
        ),
        cost_estimate=pl.CostEstimate(flops=6 * 10**9, bytes_accessed=12 * 10**6, transcendentals=0),
        name="step",
    )(*[pltpu.with_memory_space_constraint(v, pltpu.HBM) for v in (
        gate[:, 0].transpose(1, 0, 2),
        up[:, 0].transpose(1, 0, 2),
        og,
        w[0].transpose(1, 0, 2),
        m1[0].transpose(1, 0, 2),
        m2[0].transpose(1, 0, 2),
        old_map[None],
        new_map[None],
    )])
    dg, du, nf, ns, sd = pl.pallas_call(
        write_out,
        out_shape=[jax.ShapeDtypeStruct(o.shape, o.dtype) for o in outs],
        in_specs=[pl.BlockSpec(memory_space=V)] * 5,
        out_specs=[hbm] * 5,
        scratch_shapes=[pltpu.SemaphoreType.DMA((5,))],
        name="write_out",
    )(*[pltpu.with_memory_space_constraint(o, V) for o in outs])
    return (
        dg.transpose(1, 0, 2)[:, None],
        du.transpose(1, 0, 2)[:, None],
        nf.transpose(1, 0, 2)[None],
        ns.transpose(1, 0, 2)[None],
        sd.transpose(1, 0, 2)[None],
    )


def solution(mesh):
    act, state = P("dp", "owner", None, None), P("owner", "dp", None, None)
    return jax.shard_map(
        per_device,
        mesh=mesh,
        in_specs=(act, act, P("dp", None), state, state, state, P(), P()),
        out_specs=(act, act, state, state, state),
        check_vma=False,
    )
```

```python
import functools

import jax
import jax.numpy as jnp
from jax import lax
from jax.experimental import pallas as pl
from jax.experimental.pallas import tpu as pltpu
from jax.sharding import PartitionSpec as P

MESH = pl.DeviceIdType.MESH
BF, F32 = jnp.bfloat16, jnp.float32
NZ, NY, NX = 16, 4, 4
HOPS = 8
CAP, CAP_OLD, SLAB = 6, 9, 128
TOK, WIDTH = 384, 2560
HALF = WIDTH // 2
ROWS = WIDTH // 32
COLS = CAP * SLAB
SUBS = 3
SUB = COLS // SUBS
UNIT = TOK // 8
GB = 256
N_SLAB = 54
LR1, LR2 = 0.9, 0.95

RECV, SEND = {}, {}


def _number(*names):
    for n in names:
        RECV[n], SEND[n] = len(set(RECV.values())), len(set(SEND.values()))


for _s in range(HOPS):
    for _d in range(2):
        for _k in range(SUBS):
            RECV["ag", _d, _s, _k] = RECV["rs", _d, _s, _k] = (_s * 2 + _d) * SUBS + _k
            SEND["ag", _d, _s, _k] = (_s % 2 * 2 + _d) * SUBS + _k
            SEND["rs", _d, _s, _k] = 4 * SUBS + (_s % 2 * 2 + _d) * SUBS + _k
_number(("og",), ("ogx", 0), ("ogx", 1), ("ogx", 2), *[("ogc", i) for i in range(4)])
_number(*[(n, k) for n in ("hid", "hg") for k in range(SUBS)])
for _i in range(2):
    _number(("my", _i), *[("mx", j, _i) for j in range(3)], *[("mc", j, _i) for j in range(4)])


def body(
    gate, up, og, w, m1, m2, old_map, new_map,
    dg_v, du_v, nf_v, ns_v, sd_v,
    gate_v, up_v, fg, fu, m1_v, m2_v, old_v, new_v, og_s, og_v, ogt, hid, hgs, hgr, hg_own,
    wb, gb, rsb, mb, grad,
    ssem, rsem, lsem,
):
    dp, ow = lax.axis_index("dp"), lax.axis_index("owner")
    hi, z = dp // NZ, dp % NZ
    lo, x, core = ow // 8, (ow // 2) % NX, ow % 2
    y = hi * 2 + lo

    def dev(y_, x_, z_, c_):
        return ((y_ // 2) * NZ + z_, (y_ % 2) * 8 + x_ * 2 + c_)

    zn = (dev(y, x, (z + 1) % NZ, core), dev(y, x, (z + NZ - 1) % NZ, core))
    far = dev((y + 2) % NY, x, z, core)
    lows = dev((y // 2) * 2 + 1 - lo, x, z, core)
    xn = (dev(y, (x + 1) % NX, z, core), dev(y, (x + NX - 1) % NX, z, core))
    across = dev(y, (x + 2) % NX, z, core)
    cn = dev(y, x, z, 1 - core)
    other = dev((y + NY - 1 + 2 * lo) % NY, x, z, core)

    started = {}

    def copy(name, src, dst, device):
        return pltpu.make_async_remote_copy(
            src_ref=src, dst_ref=dst, send_sem=ssem.at[SEND[name]], recv_sem=rsem.at[RECV[name]],
            device_id=device, device_id_type=MESH,
        )

    def send(name, src, dst, device):
        i = SEND[name]
        if i in started:
            started[i].wait_send()
        started[i] = copy(name, src, dst, device)
        started[i].start()

    def arrived(name, dst, device):
        copy(name, dst, dst, device).wait_recv()

    def local(i, src, dst):
        return pltpu.make_async_copy(src, dst, lsem.at[i])

    def rows_of(t):
        return pl.ds(pl.multiple_of(t * ROWS, 16), ROWS)

    def sub(k):
        return pl.ds(k * SUB, SUB)

    mine_d = pl.ds(pl.multiple_of(hi * HALF, 128), HALF)
    other_d = pl.ds(pl.multiple_of((1 - hi) * HALF, 128), HALF)

    def unit(x_, c_):
        return pl.ds(pl.multiple_of((x_ * 2 + c_) * UNIT, 16), UNIT)

    barrier = pltpu.get_barrier_semaphore()
    for n in (*zn, *xn, cn, far, other, lows, across):
        pl.semaphore_signal(barrier, inc=1, device_id=n, device_id_type=MESH)

    loads_w = [local(i, w.at[i], wb.at[rows_of(z), pl.ds(i * SLAB, SLAB)]) for i in range(CAP)]
    load_gate, load_up = local(6, gate, gate_v), local(7, up, up_v)
    load_og = local(8, og.at[:, mine_d], og_v.at[pl.ds(0, TOK)])
    load_m = [local(9, m1, m1_v), local(10, m2, m2_v)]
    load_map = [local(16, old_map, old_v), local(17, new_map, new_v)]
    load_unit = local(18, og.at[unit(x, core), other_d], og_s)
    for c in [load_unit, *loads_w, load_gate, load_up, load_og, *load_m, *load_map]:
        c.start()

    pl.semaphore_wait(barrier, 9)

    def og_part(x_, c_):
        return og_v.at[pl.ds(pl.multiple_of(TOK + (x_ * 2 + c_) * UNIT, 16), UNIT)]

    load_unit.wait()
    send(("og",), og_s, og_part(x, core), other)

    def hops(d, k):
        return HOPS if d == k % 2 else HOPS - 1

    def ag_slot(d, s):
        return (z + NZ - s) % NZ if d == 0 else (z + s) % NZ

    def ag(s, *parts):
        for k in parts or range(SUBS):
            for d in range(2):
                if s > hops(d, k):
                    continue
                ref = wb.at[rows_of(ag_slot(d, s)), sub(k)]
                if s > 0:
                    arrived(("ag", d, s - 1, k), ref, zn[d])
                if s < hops(d, k):
                    send(("ag", d, s, k), ref, ref, zn[d])

    def rs_dest(d, s, k):
        n = hops(d, k)
        return (z + n - s) % NZ if d == 0 else (z + NZ - n + s) % NZ

    def rs(s, k):
        for d in range(2):
            n = hops(d, k)
            if s > n:
                continue
            if s == 0:
                src = gb.at[rows_of(rs_dest(d, s, k)), sub(k)]
            else:
                src = rsb.at[d, s - 1, :, sub(k)]
                arrived(("rs", d, s - 1, k), src, zn[d])
                if s == n:
                    continue
                mine = gb[rows_of(rs_dest(d, s, k)), sub(k)]
                src[...] = (src[...].astype(F32) + mine.astype(F32)).astype(BF)
            send(("rs", d, s, k), src, rsb.at[d, s, :, sub(k)], zn[d])

    def rs_sum(k):
        total = gb[rows_of(z), sub(k)].astype(F32)
        for d in range(2):
            total += rsb[d, hops(d, k) - 1, :, sub(k)].astype(F32)
        grad[:, sub(k)] = total * (TOK * 32) ** (-0.5)

    for c in loads_w:
        c.wait()
    ag(0, 0)

    load_gate.wait()
    load_up.wait()
    step = 64

    for slot in range(CAP):

        @pl.loop(0, TOK // step)
        def _(i):
            r = pl.ds(pl.multiple_of(i * step, step), step)
            g = gate_v[slot, r, :].astype(F32)
            u = up_v[slot, r, :].astype(F32)
            sig = jax.nn.sigmoid(g)
            gs = g * sig
            hid[r, pl.ds(slot * SLAB, SLAB)] = (gs * u).astype(BF)
            fu[slot, r, :] = gs
            fg[slot, r, :] = u * sig * (1.0 + g * (1.0 - sig))

    own, theirs = pl.ds(0, TOK), pl.ds(TOK, TOK)

    def hid_to(k, c):
        name = ("hid", k)
        started[SEND[name]] = copy(name, hid.at[own, sub(k)], hid.at[theirs, sub(k)], far)

        @pl.when(core == c)
        def _():
            started[SEND[name]].start()

    def turn(tokens):
        for i in range(HALF // GB):
            ogt[pl.ds(i * GB, GB), tokens] = og_v[tokens, pl.ds(i * GB, GB)].T

    ag(0, 1)
    load_og.wait()
    turn(own)

    x1, x2, x3 = (x + 1) % NX, (x + 2) % NX, (x + 3) % NX
    me = x * 2 + core

    def mom(x_, i):
        return mb.at[x_ * 2 + core, i]

    def mom_copies(i):
        targets = [(("mx", j, i), device) for j, device in enumerate((*xn, across))]
        return [copy(n, mom(x, i), mom(x, i), device) for n, device in (*targets, (("mc", 0, i), cn))]

    mom_y = [copy(("my", i), mom(x, i), mom(x, i), lows) for i in range(2)]

    for c in (*load_m, *load_map):
        c.wait()

    @pl.when(lo == 0)
    def _():
        @pl.loop(0, CAP_OLD)
        def _(j):
            mb[me, 0, j] = m1_v[j].astype(BF)
            mb[me, 1, j] = m2_v[j].astype(BF)

    ag(0, 2)

    def og_to(name, x_, device):
        send(name, og_part(x_, core), og_part(x_, core), device)

    ag(1, 0)
    arrived(("og",), og_part(x, core), other)
    for j, device in enumerate((*xn, across)):
        og_to(("ogx", j), x, device)
    og_to(("ogc", 0), x, cn)
    hid_to(0, 0)
    ag(1, 1, 2)
    hid_to(1, 0)
    hid_to(0, 1)
    ag(2)
    hid_to(2, 0)
    hid_to(1, 1)
    ag(3, 0)
    for j, x_ in enumerate((x3, x1, x2)):
        arrived(("ogx", j), og_part(x_, core), xn[0])
        og_to(("ogc", j + 1), x_, cn)

    @pl.when(lo == 0)
    def _():
        for c in (*mom_copies(0), *mom_copies(1)):
            c.start()

    ag(3, 1, 2)
    hid_to(2, 1)
    for j, x_ in enumerate((x, x3, x1, x2)):
        arrived(("ogc", j), og_part(x_, 1 - core), cn)
    turn(theirs)

    def gradient(k):
        arrived(("hid", k), hid.at[theirs, sub(k)], far)

        @pl.loop(0, 2)
        def _(i):
            r = pl.ds(pl.multiple_of(i * (HALF // 2), 128), HALF // 2)
            gb[r, sub(k)] = jnp.dot(
                ogt[r, :], hid[:, sub(k)], preferred_element_type=F32
            ).astype(BF)

    def mom_y_start(i):
        @pl.when(lo == 0)
        def _():
            mom_y[i].start()

    gradient(0)
    rs(0, 0)
    mom_y_start(0)
    ag(4)
    gradient(1)
    rs(1, 0)
    rs(0, 1)
    mom_y_start(1)
    gradient(2)
    rs(0, 2)
    ag(5)
    rs(2, 0)
    rs(1, 1)
    def mom_round(i):
        @pl.when(lo == 1)
        def _():
            mom_y[i].wait_recv()
            for c in mom_copies(i):
                c.start()

    ag(6)
    mom_round(0)
    rs(1, 2)
    mom_round(1)
    ag(7, 0, 1)
    rs(2, 2)
    rs(2, 1)

    def hidden_grad(tokens, k, out):
        out[:, sub(k)] = jnp.dot(
            og_v[tokens, :], wb[:, sub(k)], preferred_element_type=F32
        ).astype(out.dtype)

    def hg_to(k):
        hidden_grad(theirs, k, hgs)
        send(("hg", k), hgs.at[:, sub(k)], hgr.at[:, sub(k)], far)

    rs(3, 0)
    ag(8, 0, 1)
    for k in (2, 1):
        rs(3, k)
    hg_to(0)
    ag(7, 2)
    for k in (2, 1, 0):
        rs(4, k)
    hg_to(1)

    same = (N_SLAB, N_SLAB)
    lane, row = lax.broadcasted_iota(jnp.int32, same, 1), lax.broadcasted_iota(jnp.int32, same, 0)
    diagonal, earlier = lane == row, row < lane

    def owners_ranks(ref):
        across = jnp.broadcast_to(ref[...], same)
        down = jnp.sum(jnp.where(diagonal, across, 0), axis=1, keepdims=True)
        rank = jnp.sum(jnp.where((across == down) & earlier, 1, 0), axis=0, keepdims=True)
        return ref[...], rank

    old_own, old_rank = owners_ranks(old_v)
    new_own, new_rank = owners_ranks(new_v)
    slots = []
    for k in range(CAP):
        here = (new_own == ow) & (new_rank == k)
        slots.append(
            tuple(jnp.sum(jnp.where(here, v, 0)) for v in (old_own, old_rank, jnp.ones_like(old_own)))
        )

    ag(8, 2)
    for k in (2, 1, 0):
        rs(5, k)
    hg_to(2)

    def mom_on(j, x_):
        for i in range(2):
            arrived(("mx", j, i), mom(x_, i), xn[0])
            send(("mc", j + 1, i), mom(x_, i), mom(x_, i), cn)

    mom_on(0, x3)
    mom_on(1, x1)

    def cotangents(part):
        arrived(("hg", part), hgr.at[:, sub(part)], far)
        for k in range(part * CAP // SUBS, (part + 1) * CAP // SUBS):
            live = slots[k][2].astype(F32)

            @pl.loop(0, TOK // step)
            def _(i):
                r = pl.ds(pl.multiple_of(i * step, step), step)
                c = pl.ds(k * SLAB, SLAB)
                hg = (hg_own[r, c] + hgr[r, c].astype(F32)) * live
                dg_v[k, r, :] = (hg * fg[k, r, :]).astype(BF)
                du_v[k, r, :] = (hg * fu[k, r, :]).astype(BF)

    for k in (2, 1, 0):
        rs(6, k)
    hidden_grad(own, 0, hg_own)
    mom_on(2, x2)
    cotangents(0)
    for k in (2, 1, 0):
        rs(7, k)
    for k in (1, 2):
        hidden_grad(own, k, hg_own)
        cotangents(k)
    def adam(part):
        for k in range(part * CAP // SUBS, (part + 1) * CAP // SUBS):
            q, j, n = slots[k]
            live = n.astype(F32)
            g = grad[:, pl.ds(k * SLAB, SLAB)]
            m = (LR1 * mb[q, 0, j].astype(F32) + 0.1 * g) * live
            s = (LR2 * mb[q, 1, j].astype(F32) + 0.05 * g * g) * live
            nf_v[k] = m
            ns_v[k] = s
            sd_v[k] = m / (1.0 - LR1**20) / (jnp.sqrt(s / (1.0 - LR2**20)) + 1e-08)

    for j, x_ in enumerate((x, x3, x1, x2)):
        for i in range(2):
            ref = mb.at[x_ * 2 + 1 - core, i]
            arrived(("mc", j, i), ref, cn)
    for k in (2, 1, 0):
        rs(8, k)
        rs_sum(k)
        adam(k)

    @pl.when(lo == 0)
    def _():
        for c in mom_y:
            c.wait_send()

    for c in (*started.values(), *mom_copies(0), *mom_copies(1)):
        c.wait_send()


def write_out(*refs):
    src, dst, sem = refs[:5], refs[5:10], refs[10]
    copies = [pltpu.make_async_copy(src[i], dst[i], sem.at[i]) for i in range(5)]
    for c in copies:
        c.start()
    for c in copies:
        c.wait()


def per_device(gate, up, og, w, m1, m2, old_map, new_map):
    hbm = pl.BlockSpec(memory_space=pl.ANY)
    act = (CAP, TOK, SLAB)
    state = (CAP, ROWS, SLAB)
    old = (CAP_OLD, ROWS, SLAB)
    V = pltpu.VMEM
    outs = pl.pallas_call(
        body,
        out_shape=[V(act, BF)] * 2 + [V(state, F32)] * 3,
        in_specs=[hbm] * 8,
        out_specs=[pl.BlockSpec(memory_space=V)] * 5,
        scratch_shapes=[
            V(act, BF), V(act, BF), V(act, F32), V(act, F32), V(old, F32), V(old, F32), V((1, N_SLAB), jnp.int32), V((1, N_SLAB), jnp.int32),
            V((UNIT, HALF), BF), V((2 * TOK, HALF), BF), V((HALF, 2 * TOK), BF), V((2 * TOK, COLS), BF),
            V((TOK, COLS), BF), V((TOK, COLS), BF), V((TOK, COLS), F32),
            V((HALF, COLS), BF), V((HALF, COLS), BF), V((2, HOPS, ROWS, COLS), BF),
            V((8, 2, *old), BF), V((ROWS, COLS), F32),
            pltpu.SemaphoreType.DMA((len(set(SEND.values())),)),
            pltpu.SemaphoreType.DMA((len(set(RECV.values())),)),
            pltpu.SemaphoreType.DMA((19,)),
        ],
        compiler_params=pltpu.CompilerParams(
            collective_id=0, has_side_effects=True, vmem_limit_bytes=40 << 20
        ),
        cost_estimate=pl.CostEstimate(flops=6 * 10**9, bytes_accessed=12 * 10**6, transcendentals=0),
        name="step",
    )(*[pltpu.with_memory_space_constraint(v, pltpu.HBM) for v in (
        gate[:, 0].transpose(1, 0, 2),
        up[:, 0].transpose(1, 0, 2),
        og,
        w[0].transpose(1, 0, 2),
        m1[0].transpose(1, 0, 2),
        m2[0].transpose(1, 0, 2),
        old_map[None],
        new_map[None],
    )])
    dg, du, nf, ns, sd = pl.pallas_call(
        write_out,
        out_shape=[jax.ShapeDtypeStruct(o.shape, o.dtype) for o in outs],
        in_specs=[pl.BlockSpec(memory_space=V)] * 5,
        out_specs=[hbm] * 5,
        scratch_shapes=[pltpu.SemaphoreType.DMA((5,))],
        name="write_out",
    )(*[pltpu.with_memory_space_constraint(o, V) for o in outs])
    return (
        dg.transpose(1, 0, 2)[:, None],
        du.transpose(1, 0, 2)[:, None],
        nf.transpose(1, 0, 2)[None],
        ns.transpose(1, 0, 2)[None],
        sd.transpose(1, 0, 2)[None],
    )


def solution(mesh):
    act, state = P("dp", "owner", None, None), P("owner", "dp", None, None)
    return jax.shard_map(
        per_device,
        mesh=mesh,
        in_specs=(act, act, P("dp", None), state, state, state, P(), P()),
        out_specs=(act, act, state, state, state),
        check_vma=False,
    )
```
